32 devices in a mesh: doc: 4 (over x, core), term: 8 (over z, y).
Axes of the slice: x: 2, y: 2, z: 4, core: 2. Of those that a mesh axis runs over, the one named last changes fastest.
Arguments:
- query_states: bfloat16 [256, 32, 768], P('doc'), may hold values from -6 to 6
- token_ids: int32 [256, 32], P('doc'), may hold values from 0 to 30521, as said below
- transform_weight: bfloat16 [768, 768], replicated, may hold values from -0.21875 to 0.21875
- transform_bias: float32 [768], replicated, may hold values from -3 to 3
- norm_gain: float32 [768], replicated, may hold values from 0.5 to 1.5
- norm_bias: float32 [768], replicated, may hold values from -3 to 3
- decoder_weight: bfloat16 [768, 30720], P(None, 'term'), may hold values from -0.21875 to 0.21875
- decoder_bias: float32 [30720], P('term'), may hold values from -2.5 to 0.5
- candidates: int32 [256, 32], P('doc'), may hold values from 0 to 63, all different within a row; in each aligned block of 64 rows (0 to 63, 64 to 127, ...) at most 32 rows name the same one
- occupancy: int32 [64, 240], P('doc', 'term'), may hold values 0 or 1
- doc_blocks: bfloat16 [64, 240, 128, 128], P('doc', 'term'), may hold values from -0.046875 to 0.046875
Outputs:
- query_weights: bfloat16 [256, 30720], P('doc', 'term')
- scores: float32 [256, 32, 128], P('doc', None, 'term')
The draws below stay inside these ranges and needn't reach their ends.
Inputs may be any that keep to these rules, and one draw needn't show every extreme that they name: `token_ids`: id 0 marks padding: a query has non-zero ids at its first positions, at least 8 of them, and 0 after them. `candidates`: A query names 32 different tiles; among the 64 queries of one doc index no tile is named by more than 32 of them.
All inputs are finite; a program needn't handle non-finite values. No bound on the sum of `occupancy` on one device may be relied on, other than what follows from the above.
Results may differ from the reference program's by a relative error of at most 0.0041.
Values may be sent and summed in bfloat16 or wider, within the bound.
No kernel may reach another device: no remote copies, remote signals or barrier semaphores. Data moves between devices by JAX's collectives and lax.ppermute only.
A program may use at most 128 MiB of HBM per device.

```python
import math
import jax
import jax.numpy as jnp
import numpy as np
from jax import lax

DM = 768
VOCAB = 30522
BS = 128
TB = 240
TILE = 128
Q_DEV = 64
QLEN = 32
CAND = 32
MOST = 32
VP = 30720
NT = 64
QUERIES = 256
N_DOC = 4


def draw_token_ids(key, part):
    length_key, token_key = jax.random.split(key)
    lengths = jax.random.randint(length_key, (QUERIES, 1), max(1, QLEN // 4), QLEN + 1)
    tokens = jax.random.randint(token_key, (QUERIES, QLEN), 1, VOCAB)
    position = lax.iota(jnp.int32, QLEN)[None, :]
    return jnp.where(position < lengths, tokens, 0).astype(jnp.int32)


def plant(array, key, least, top_value):
    longest = array.shape.index(max(array.shape))
    spots = []
    for shift in (0, 1):
        where = [jax.random.randint(jax.random.fold_in(key, axis), (), 0, length) for axis, length in enumerate(array.shape)]
        where[longest] = (where[longest] + shift) % array.shape[longest]
        spots.append(tuple(where))
    return array.at[spots[0]].set(least).at[spots[1]].set(top_value)


def with_spikes(values, stream_key, source, target, blocks, factor):
    owner, partner = [(jnp.arange(values.shape[dim]) // (values.shape[dim] // blocks)).reshape([-1 if axis == dim else 1 for axis in range(values.ndim)]) for dim in (source, target)]
    chosen = jax.random.permutation(stream_key, blocks)[partner]
    strong = (owner == chosen) | (owner == (partner + blocks // 2) % blocks)
    return jnp.where(strong, factor * values, values)


def block_scale(own_key, dims, pieces, smallest, top_value):
    gain, own = 1.0, jax.random.fold_in(own_key, 6)
    for dim, blocks in pieces:
        heights = jnp.exp(jax.random.uniform(jax.random.fold_in(own, dim), (blocks,), jnp.float32, smallest / len(pieces), top_value / len(pieces)))
        gain = gain * jnp.repeat(heights, dims[dim] // blocks).reshape([-1 if axis == dim else 1 for axis in range(len(dims))])
    return gain


def deal_out(stream_key, own, number, rows, count, top, reach, lean):
    sequence = jax.random.permutation(stream_key, count)
    heavy_load, ordinary = portions_of(count, rows * top, reach, lean, True), portions_of(count, rows * top, reach, lean, False)
    places = jnp.arange(count)

    def named(sizes, offset_by):
        used = int((sizes > 0).sum())
        fixed = max(1, used // 4)
        moved = fixed + (places - fixed + offset_by * (used - fixed)) % max(1, count - fixed)
        return jnp.zeros((count,), jnp.int32).at[sequence[jnp.where(places < fixed, places, moved)]].set(jnp.asarray(sizes, jnp.int32))

    sizes = jnp.where(number % 4 == 0, named(heavy_load, number // 4), named(ordinary, number - number // 4 - 1))
    mixed = jax.random.permutation(jax.random.fold_in(own, 3), count)
    source_of, taker = mixed[0:count // 2 * 2:2], mixed[1:count // 2 * 2:2]
    slack = jnp.minimum(sizes[source_of] - 1, reach - sizes[taker]) // 2
    slack = jnp.where((source_of == sequence[0]) | (taker == sequence[0]) | (sizes[taker] == 0), 0, jnp.maximum(slack, 0))
    moved = jax.random.randint(jax.random.fold_in(own, 4), (count // 2,), 0, 1 << 20) % (slack + 1)
    sizes = sizes.at[source_of].add(-moved).at[taker].add(moved)
    items = jnp.searchsorted(jnp.cumsum(sizes), jnp.arange(rows * top), side="right").astype(jnp.int32)
    table = items.reshape(top, rows).T
    table = table[jax.random.permutation(jax.random.fold_in(own, 1), rows)]
    offset_by = jax.random.randint(jax.random.fold_in(own, 2), (rows, 1), 0, top)
    return jnp.take_along_axis(table, (jnp.arange(top)[None, :] + offset_by) % top, axis=1)


def portions_of(count, total, limit, skew, full):
    portions = [(1 << 20) // math.isqrt(grade ** skew) + 1 for grade in range(1, count + 1)]
    largest = limit if full else min(limit, max(-(-total // count), total * portions[0] // sum(portions)))
    least = 1 if total - largest >= count - 1 else 0
    counts, rest = [largest] + [least] * (count - 1), total - largest - least * (count - 1)
    while rest > 0:
        free = [i for i in range(1, count) if counts[i] < largest] or [i for i in range(1, count) if counts[i] < limit]
        whole, remaining = sum([portions[i] for i in free]), rest
        for i in free:
            extra = min(limit - counts[i], max(1, remaining * portions[i] // whole), rest)
            counts[i] = counts[i] + extra
            rest = rest - extra
    return np.array(counts)


def gaussian(stream_key, dims, scale, most, cuts=(), kind=jnp.bfloat16):
    factor_of = block_scale(stream_key, dims, cuts, -0.22, 0.18) if cuts else 1.0
    entries = jax.random.normal(stream_key, dims, jnp.float32) * scale * factor_of
    return jnp.minimum(jnp.maximum(entries, -most), most).astype(kind)


def bell_draw_with(rng, shape, width, bound, cuts, heavy, dtype=jnp.bfloat16):
    result = width * jax.random.normal(rng, shape, jnp.float32)
    if cuts:
        result = result * block_scale(rng, shape, cuts, -0.22, 0.18)
    return jnp.clip(with_spikes(result, jax.random.fold_in(rng, 3), *heavy), -bound, bound).astype(dtype)


def setup_inputs(seed: int = 0) -> dict:
    seeds = jax.random.split(jax.random.key(seed), 12)
    query_states = gaussian(seeds[0], (QUERIES, QLEN, DM), 1.0, 6.0, ((0, 4),))
    token_ids = draw_token_ids(jax.random.fold_in(seeds[11], 71), 0)
    transform_weight = gaussian(seeds[2], (DM, DM), DM ** -0.5, 0.21875)
    transform_bias = gaussian(seeds[3], (DM,), 0.5, 3.0, (), jnp.float32)
    norm_gain = jnp.clip(1.0 + 0.1 * jax.random.normal(seeds[4], (DM,), jnp.float32), 0.5, 1.5)
    norm_bias = gaussian(seeds[5], (DM,), 0.5, 3.0, (), jnp.float32)
    decoder_weight = gaussian(seeds[6], (DM, VP), DM ** -0.5, 0.21875, ((1, 8),))
    decoder_bias = jnp.clip(-2.5 + 3.0 * jax.random.uniform(seeds[7], (VP,), jnp.float32) ** block_scale(seeds[7], (VP,), ((0, 8),), -0.2, 0.2), -2.5, 0.5)
    candidates_keys = jax.random.split(jax.random.fold_in(seeds[8], 1), QUERIES // Q_DEV)
    candidates_turns = jax.random.permutation(jax.random.fold_in(seeds[8], 3), QUERIES // Q_DEV)
    candidates = jax.vmap(lambda own, number: deal_out(jax.random.fold_in(seeds[8], 2), own, number, Q_DEV, NT, CAND, MOST, 2))(candidates_keys, candidates_turns).reshape((QUERIES, CAND))
    occupancy = plant((jax.random.randint(seeds[9], (NT, TB), 0, 4) < 3).astype(jnp.int32), jax.random.fold_in(seeds[9], 1), 0, 1)
    doc_blocks = bell_draw_with(seeds[10], (NT, TB, TILE, BS), VOCAB ** -0.5, 0.046875, ((0, 4), (1, 8)), (1, 2, 8, 2.0))
    return {"query_states": query_states, "token_ids": token_ids, "transform_weight": transform_weight, "transform_bias": transform_bias, "norm_gain": norm_gain, "norm_bias": norm_bias, "decoder_weight": decoder_weight, "decoder_bias": decoder_bias, "candidates": candidates, "occupancy": occupancy, "doc_blocks": doc_blocks}


def expand(states, token_mask, transform_weight, transform_bias, norm_gain, norm_bias, decoder_weight, decoder_bias):
    query_count, query_length, model_width = states.shape
    hidden = jnp.dot(states.reshape(query_count * query_length, model_width), transform_weight, preferred_element_type=jnp.float32) + transform_bias
    hidden = jax.nn.gelu(hidden, approximate=False)
    centred = hidden - lax.optimization_barrier(jnp.mean(hidden, axis=-1, keepdims=True))
    spread = lax.optimization_barrier(jnp.mean(centred * centred, axis=-1, keepdims=True))
    normed = (centred * lax.rsqrt(spread + 1e-06) * norm_gain + norm_bias).astype(jnp.bfloat16)
    logits = jnp.dot(normed, decoder_weight, preferred_element_type=jnp.float32) + decoder_bias
    activated = jnp.log1p(jnp.maximum(logits, 0.0)).reshape(query_count, query_length, -1)
    live_mask = (token_mask != 0).astype(jnp.float32)[:, :, None]
    return lax.optimization_barrier(jnp.max(activated * live_mask, axis=1))

def reference(query_states, token_ids, transform_weight, transform_bias, norm_gain, norm_bias, decoder_weight, decoder_bias, candidates, occupancy, doc_blocks):
    state_blocks = query_states.reshape(N_DOC, Q_DEV, QLEN, DM)
    id_blocks = token_ids.reshape(N_DOC, Q_DEV, QLEN)

    def expand_block(packed):
        return expand(packed[0], packed[1], transform_weight, transform_bias, norm_gain, norm_bias, decoder_weight, decoder_bias)
    pooled = lax.map(expand_block, (state_blocks, id_blocks)).reshape(QUERIES, VP)
    vocab_keep = (lax.iota(jnp.int32, VP) < VOCAB).astype(jnp.float32)
    weights = (pooled * vocab_keep).astype(jnp.bfloat16)
    tile_index = lax.iota(jnp.int32, NT)
    tile_hits = lax.optimization_barrier(jnp.sum((candidates[:, :, None] == tile_index[None, None, :]).astype(jnp.int32), axis=1)).reshape(N_DOC, Q_DEV, NT)
    tile_before = jnp.cumsum(tile_hits, axis=1) - tile_hits
    hits_by_tile = jnp.transpose(tile_hits, (2, 0, 1))
    before_by_tile = jnp.transpose(tile_before, (2, 0, 1))
    slot_index = lax.iota(jnp.int32, MOST)
    row_index = lax.iota(jnp.int32, Q_DEV)
    block_start = lax.iota(jnp.int32, N_DOC)[:, None] * Q_DEV

    def tile_scores(packed):
        one_hits, one_before, one_block, one_occupied = packed
        chosen = (one_hits[:, None, :] > 0) & (one_before[:, None, :] == slot_index[None, :, None])
        source_row = lax.optimization_barrier(jnp.sum(jnp.where(chosen, row_index[None, None, :], 0), axis=-1))
        slot_valid = jnp.any(chosen, axis=-1).astype(jnp.float32)
        flat_index = (block_start + source_row).reshape(-1)
        gathered = jnp.take(weights, flat_index, axis=0).astype(jnp.float32).reshape(N_DOC, MOST, TB, BS)
        gathered = gathered * slot_valid[:, :, None, None] * one_occupied.astype(jnp.float32)[None, None, :, None]
        return jnp.einsum('jrbc,bdc->jrd', gathered, one_block.astype(jnp.float32), precision=lax.Precision.HIGHEST)
    table = lax.map(tile_scores, (hits_by_tile, before_by_tile, doc_blocks, occupancy))
    slot_rank = jnp.take_along_axis(tile_before.reshape(QUERIES, NT), candidates, axis=1)
    owner = (lax.iota(jnp.int32, QUERIES) // Q_DEV)[:, None]
    flat_index = (candidates * N_DOC + owner) * MOST + slot_rank
    scores = jnp.take(table.reshape(-1, TILE), flat_index.reshape(-1), axis=0).reshape(QUERIES, CAND, TILE)
    return (weights, scores)
```

```python
import functools
import math

import jax
import jax.numpy as jnp
from jax import lax
from jax.experimental import pallas as pl
from jax.experimental.pallas import tpu as pltpu
from jax.sharding import PartitionSpec as P

VOCAB = 30522
MOST = 32
LANES = 128
GROUP = 8
F32 = jnp.float32
BF16 = jnp.bfloat16
WHOLE = pl.BlockSpec(memory_space=pltpu.VMEM)
SCALARS = pl.BlockSpec(memory_space=pltpu.SMEM)


def gelu(value):
    return 0.5 * value * (1.0 + lax.erf(value * math.sqrt(0.5)))


def normed_rows(states, live_at, first, transform, bias, gain, shift):
    queries, length, width = states.shape
    rows = queries * length
    row = lax.broadcasted_iota(jnp.int32, live_at.shape, 0)
    lane = lax.broadcasted_iota(jnp.int32, live_at.shape, 1)
    own = jnp.where(lane == first + row % queries, live_at, 0.0)
    live = jnp.sum(own, axis=1, keepdims=True) > 0.0
    row = lax.broadcasted_iota(jnp.int32, (rows, 1), 0)
    source = row % queries * length + jnp.where(live, row // queries, 0)
    column = lax.broadcasted_iota(jnp.int32, (rows, rows), 1)
    order = jnp.where(column == source, 1.0, 0.0).astype(BF16)
    moved = jnp.dot(order, states.reshape(rows, width), preferred_element_type=F32)
    hidden = jnp.dot(moved.astype(BF16), transform, preferred_element_type=F32)
    hidden = gelu(hidden + bias)
    centred = hidden - jnp.mean(hidden, axis=1, keepdims=True)
    spread = jnp.mean(centred * centred, axis=1, keepdims=True)
    return (centred * lax.rsqrt(spread + 1e-06) * gain + shift).astype(BF16)


def expand_kernel(
    piece,
    start_ref,
    states_ref,
    tokens_ref,
    transform_ref,
    bias_ref,
    gain_ref,
    shift_ref,
    decoder_ref,
    decoder_bias_ref,
    cand_ref,
    out_ref,
    pooled,
):
    length, query_total = tokens_ref.shape
    vocab = decoder_ref.shape[1]
    rows = GROUP * length
    at = lax.broadcasted_iota(jnp.int32, (rows, length), 0) // GROUP
    spot = lax.broadcasted_iota(jnp.int32, (rows, length), 1)
    pick = jnp.where(at == spot, 1.0, 0.0).astype(BF16)
    alive = jnp.where(tokens_ref[...] != 0, 1.0, 0.0).astype(BF16)
    live_at = jnp.dot(pick, alive, preferred_element_type=F32)
    count = out_ref.shape[0]
    step = 768 if vocab % 768 == 0 else 640
    for group in range(count // GROUP):
        first = piece * count + group * GROUP
        normed = normed_rows(
            states_ref[first : first + GROUP],
            live_at,
            first,
            transform_ref[...],
            bias_ref[...],
            gain_ref[...],
            shift_ref[...],
        )
        for begin in range(0, vocab, step):
            part = slice(begin, begin + step)
            logits = jnp.dot(normed, decoder_ref[:, part], preferred_element_type=F32)
            top = jnp.max(logits.reshape(length, GROUP, step), axis=0)
            top = jnp.log1p(jnp.maximum(top + decoder_bias_ref[:, part], 0.0))
            pooled[group * GROUP : (group + 1) * GROUP, part] = top
    column = start_ref[0] + lax.broadcasted_iota(jnp.int32, (count, vocab), 1)
    out_ref[:, :vocab] = jnp.where(column < VOCAB, pooled[...], 0.0).astype(BF16)
    if out_ref.shape[1] > vocab:
        wide = jnp.zeros((count, LANES), F32)
        wide = jnp.concatenate(
            [cand_ref[...].astype(F32), jnp.zeros((count, LANES - query_total), F32)], axis=1
        )
        out_ref[:, vocab:] = wide.astype(BF16)


def ranks(cand, tiles, base):
    depth, total = cand.shape
    row = lax.broadcasted_iota(jnp.int32, (tiles, total), 0) + base
    hits = jnp.zeros((tiles, total), F32)
    for place in range(depth):
        hits = jnp.where(cand[place : place + 1, :] == row, 1.0, hits)
    earlier = lax.broadcasted_iota(jnp.int32, (total, total), 0)
    later = lax.broadcasted_iota(jnp.int32, (total, total), 1)
    block = 64
    ahead = (earlier < later) & (earlier // block == later // block)
    before = jnp.dot(
        hits.astype(BF16), jnp.where(ahead, 1.0, 0.0).astype(BF16), preferred_element_type=F32
    )
    return jnp.where(hits > 0.0, before, -1.0)


def score_kernel(parties, pieces, place_ref, occupancy_ref, docs_ref, *refs):
    piece_refs = refs[: parties * pieces]
    out_ref, turned, rank, total = refs[parties * pieces :]
    step = pl.program_id(0)
    tiles, blocks, docs, terms = docs_ref.shape
    vocab = blocks * terms
    term_count = out_ref.shape[1]
    share = docs // term_count
    each = piece_refs[0].shape[0]
    queries = each * pieces

    @pl.when(step == 0)
    def _():
        cands = []
        for party in range(parties):
            weights = jnp.concatenate(
                [piece_refs[party * pieces + k][:, :vocab] for k in range(pieces)], axis=0
            )
            cands.append(piece_refs[party * pieces][:, vocab : vocab + queries].astype(F32))
            turned[party * queries : (party + 1) * queries, :] = weights
        cand = jnp.concatenate(cands, axis=1).astype(jnp.int32)
        rank[...] = ranks(cand, rank.shape[0], place_ref[0] * rank.shape[0])

    rows = []
    for tile in range(tiles):
        row = [
            jnp.where(occupancy_ref[step * tiles + tile, block] != 0, docs_ref[tile, block], 0.0).astype(BF16)
            for block in range(blocks)
        ]
        rows.append(jnp.concatenate(row, axis=1))
    left = jnp.concatenate(rows, axis=0)
    value = lax.dot_general(
        left, turned[...], (((1,), (1,)), ((), ())), preferred_element_type=F32
    ).astype(BF16)
    all_queries = parties * queries
    slot = lax.broadcasted_iota(jnp.int32, (parties * LANES, all_queries), 0)
    owner = lax.broadcasted_iota(jnp.int32, (parties * LANES, all_queries), 1) // queries
    chosen = jnp.zeros((docs, parties * LANES), F32)
    for tile in range(tiles):
        want = rank[pl.ds(step * tiles + tile, 1), :].astype(jnp.int32)
        want = jnp.where(want >= 0, want + tile * MOST, -1)
        goal = jnp.where(want >= 0, want + owner * LANES, -1)
        hot = jnp.where(slot == goal, 1.0, 0.0).astype(BF16)
        chosen = chosen + lax.dot_general(
            value[tile * docs : (tile + 1) * docs],
            hot,
            (((1,), (1,)), ((), ())),
            preferred_element_type=F32,
        )
    for party in range(parties):
        part = chosen[:, party * LANES : (party + 1) * LANES]
        for term in range(term_count):
            total[party, term, pl.ds(step * share, share), :] = part[term * share : (term + 1) * share]

    @pl.when(step == pl.num_programs(0) - 1)
    def _():
        for party in range(parties):
            out_ref[place_ref[0] ^ party] = total[party].astype(BF16)


def final_kernel(cand_ref, got_ref, out_ref):
    docs_n, term_count, rows, _ = got_ref.shape
    depth, share, queries = out_ref.shape
    groups = rows // share
    tiles = LANES // MOST
    all_tiles = docs_n * groups * tiles
    cand = cand_ref[...]
    rank = ranks(cand, all_tiles, 0)
    slot = lax.broadcasted_iota(jnp.int32, (LANES, tiles * queries), 0)
    twice = jnp.concatenate([cand, cand], axis=1)
    lane = lax.broadcasted_iota(jnp.int32, (1, 2 * queries), 1) // queries
    result = [jnp.zeros((share, 2 * queries), F32) for _ in range(depth)]
    for doc in range(docs_n):
        summed = got_ref[doc, 0].astype(F32)
        for term in range(1, term_count):
            summed = summed + got_ref[doc, term].astype(F32)
        for group in range(groups):
            first = (doc * groups + group) * tiles
            want = jnp.concatenate(
                [
                    jnp.where(rank[first + k : first + k + 1] >= 0.0, rank[first + k : first + k + 1] + k * MOST, -1.0)
                    for k in range(tiles)
                ],
                axis=1,
            ).astype(jnp.int32)
            hot = jnp.where(slot == want, 1.0, 0.0).astype(BF16)
            value = summed[group * share : (group + 1) * share]
            high = value.astype(BF16)
            low = (value - high.astype(F32)).astype(BF16)
            moved = jnp.dot(high, hot, preferred_element_type=F32) + jnp.dot(
                low, hot, preferred_element_type=F32
            )
            for pair in range(tiles // 2):
                held = moved[:, pair * 2 * queries : (pair + 1) * 2 * queries]
                name = first + pair * 2 + lane
                for place in range(depth):
                    result[place] = jnp.where(twice[place : place + 1] == name, held, result[place])
    for place in range(depth):
        out_ref[place] = result[place][:, :queries] + result[place][:, queries:]


def body(
    query_states,
    token_ids,
    transform_weight,
    transform_bias,
    norm_gain,
    norm_bias,
    decoder_weight,
    decoder_bias,
    candidates,
    occupancy,
    doc_blocks,
):
    query_count, length, width = query_states.shape
    vocab = decoder_weight.shape[1]
    tile_local, blocks, docs, terms = doc_blocks.shape
    depth = candidates.shape[1]
    term_index, doc_index = lax.axis_index("term"), lax.axis_index("doc")
    doc_count, term_count = lax.axis_size("doc"), lax.axis_size("term")
    pieces = 2
    each = query_count // pieces
    share = docs // term_count
    cand = candidates.T
    start = (term_index * vocab).reshape(1)
    place = doc_index.reshape(1)

    own = []
    for piece in range(pieces):
        wide = vocab + (LANES if piece == 0 else 0)
        own.append(
            pl.pallas_call(
                functools.partial(expand_kernel, piece),
                in_specs=[SCALARS] + [WHOLE] * 9,
                out_specs=WHOLE,
                out_shape=jax.ShapeDtypeStruct((each, wide), BF16),
                scratch_shapes=[pltpu.VMEM((each, vocab), F32)],
                cost_estimate=pl.CostEstimate(
                    flops=2 * each * length * width * (vocab + width), bytes_accessed=10**7, transcendentals=0
                ),
                compiler_params=pltpu.CompilerParams(vmem_limit_bytes=24 << 20),
                name="expand",
            )(
                start,
                query_states,
                token_ids.T,
                transform_weight,
                transform_bias.reshape(1, -1),
                norm_gain.reshape(1, -1),
                norm_bias.reshape(1, -1),
                decoder_weight,
                decoder_bias.reshape(1, -1),
                cand,
            )
        )

    held = [[None] * pieces for _ in range(doc_count)]
    for piece in range(pieces):
        held[0][piece] = own[piece]
        bit = doc_count // 2
        known = [0]
        while bit:
            swap = [(i, i ^ bit) for i in range(doc_count)]
            for k in list(known):
                held[k | bit][piece] = lax.ppermute(held[k][piece], "doc", swap)
                known.append(k | bit)
            bit //= 2
    weights = jnp.concatenate([own[0][:, :vocab], own[1]], axis=0)

    tiles = LANES // MOST
    steps = tile_local // tiles
    all_queries = doc_count * query_count
    sent = pl.pallas_call(
        functools.partial(score_kernel, doc_count, pieces),
        grid=(steps,),
        in_specs=[SCALARS, SCALARS, pl.BlockSpec((tiles, blocks, docs, terms), lambda i: (i, 0, 0, 0))]
        + [WHOLE] * (doc_count * pieces),
        out_specs=pl.BlockSpec((doc_count, term_count, steps * share, LANES), lambda i: (0, 0, 0, 0)),
        out_shape=jax.ShapeDtypeStruct((doc_count, term_count, steps * share, LANES), BF16),
        scratch_shapes=[
            pltpu.VMEM((all_queries, vocab), BF16),
            pltpu.VMEM((tile_local, all_queries), F32),
            pltpu.VMEM((doc_count, term_count, steps * share, LANES), F32),
        ],
        cost_estimate=pl.CostEstimate(
            flops=2 * tile_local * docs * vocab * all_queries, bytes_accessed=2 * 10**7, transcendentals=0
        ),
        compiler_params=pltpu.CompilerParams(vmem_limit_bytes=36 << 20),
        name="score",
    )(place, occupancy, doc_blocks, *[held[k][piece] for k in range(doc_count) for piece in range(pieces)])

    everyone = doc_count * term_count
    got = lax.all_to_all(
        sent.reshape(everyone, steps * share, LANES), ("doc", "term"), split_axis=0, concat_axis=0, tiled=True
    ).reshape(doc_count, term_count, steps * share, LANES)

    scores = pl.pallas_call(
        final_kernel,
        in_specs=[WHOLE, WHOLE],
        out_specs=WHOLE,
        out_shape=jax.ShapeDtypeStruct((depth, share, query_count), F32),
        compiler_params=pltpu.CompilerParams(vmem_limit_bytes=24 << 20),
        name="place",
    )(cand, got)
    return weights, scores.transpose(2, 0, 1)


def solution(mesh):
    placed = (
        P("doc", None, None),
        P("doc", None),
        P(),
        P(),
        P(),
        P(),
        P(None, "term"),
        P("term"),
        P("doc", None),
        P("doc", "term"),
        P("doc", "term", None, None),
    )
    return jax.shard_map(
        body,
        mesh=mesh,
        in_specs=placed,
        out_specs=(P("doc", "term"), P("doc", None, "term")),
        check_vma=False,
    )
```

```python
import functools
import math

import jax
import jax.numpy as jnp
from jax import lax
from jax.experimental import pallas as pl
from jax.experimental.pallas import tpu as pltpu
from jax.sharding import PartitionSpec as P

VOCAB = 30522
MOST = 32
LANES = 128
GROUP = 8
F32 = jnp.float32
BF16 = jnp.bfloat16
WHOLE = pl.BlockSpec(memory_space=pltpu.VMEM)
FAR = pl.BlockSpec(memory_space=pltpu.HBM)
LIMIT = 8 << 20
SCALARS = pl.BlockSpec(memory_space=pltpu.SMEM)


def gelu(value):
    return 0.5 * value * (1.0 + lax.erf(value * math.sqrt(0.5)))


def normed_rows(states, live_at, first, transform, bias, gain, shift):
    queries, length, width = states.shape
    rows = queries * length
    row = lax.broadcasted_iota(jnp.int32, live_at.shape, 0)
    lane = lax.broadcasted_iota(jnp.int32, live_at.shape, 1)
    own = jnp.where(lane == first + row % queries, live_at, 0.0)
    live = jnp.sum(own, axis=1, keepdims=True) > 0.0
    row = lax.broadcasted_iota(jnp.int32, (rows, 1), 0)
    source = row % queries * length + jnp.where(live, row // queries, 0)
    column = lax.broadcasted_iota(jnp.int32, (rows, rows), 1)
    order = jnp.where(column == source, 1.0, 0.0).astype(BF16)
    moved = jnp.dot(order, states.reshape(rows, width), preferred_element_type=F32)
    hidden = jnp.dot(moved.astype(BF16), transform, preferred_element_type=F32)
    hidden = gelu(hidden + bias)
    centred = hidden - jnp.mean(hidden, axis=1, keepdims=True)
    spread = jnp.mean(centred * centred, axis=1, keepdims=True)
    return (centred * lax.rsqrt(spread + 1e-06) * gain + shift).astype(BF16)


def place_of(rows, live_at, tokens_ref):
    length = tokens_ref.shape[0]
    at = lax.broadcasted_iota(jnp.int32, (rows, length), 0) // GROUP
    spot = lax.broadcasted_iota(jnp.int32, (rows, length), 1)
    pick = jnp.where(at == spot, 1.0, 0.0).astype(BF16)
    alive = jnp.where(tokens_ref[...] != 0, 1.0, 0.0).astype(BF16)
    live_at[...] = jnp.dot(pick, alive, preferred_element_type=F32)


def pool(rows, decoder_ref, bias_ref, group, length, out_ref):
    logits = jnp.dot(rows, decoder_ref[...], preferred_element_type=F32)
    top = jnp.max(logits.reshape(length, GROUP, logits.shape[1]), axis=0)
    out_ref[group * GROUP : (group + 1) * GROUP, :] = jnp.log1p(
        jnp.maximum(top + bias_ref[...], 0.0)
    )


def keep_vocab(start, pooled):
    column = start + lax.broadcasted_iota(jnp.int32, pooled.shape, 1)
    return jnp.where(column < VOCAB, pooled[...], 0.0).astype(BF16)


def first_kernel(
    start_ref,
    states_hbm,
    tokens_hbm,
    transform_hbm,
    bias_hbm,
    gain_hbm,
    shift_hbm,
    decoder_hbm,
    decoder_bias_hbm,
    cand_hbm,
    out_ref,
    normed_ref,
    next_ref,
    decoder_bias_ref,
    states_ref,
    transform_ref,
    decoder_ref,
    bias_ref,
    gain_ref,
    shift_ref,
    tokens_ref,
    cand_ref,
    live_at,
    pooled,
    sems,
):
    queries, length, _ = states_ref.shape
    groups = queries // GROUP
    rows = GROUP * length
    chunk = decoder_ref.shape[1]
    always = start_ref[0] >= 0
    copies = []

    def bring(source, target):
        copy = pltpu.make_async_copy(source, target, sems.at[len(copies)])
        copies.append(copy)
        copy.start()

    half = pl.ds(0, 2 * GROUP)
    other = pl.ds(2 * GROUP, queries - 2 * GROUP)
    bring(tokens_hbm, tokens_ref)
    bring(bias_hbm, bias_ref.at[0])
    bring(gain_hbm, gain_ref.at[0])
    bring(shift_hbm, shift_ref.at[0])
    bring(states_hbm.at[half], states_ref.at[half])
    bring(transform_hbm, transform_ref)
    early = len(copies)
    bring(decoder_hbm.at[:, pl.ds(0, chunk)], decoder_ref)
    for at in range(decoder_bias_ref.shape[0]):
        bring(decoder_bias_hbm.at[pl.ds(at * chunk, chunk)], decoder_bias_ref.at[at, 0])
    bring(states_hbm.at[other], states_ref.at[other])
    bring(cand_hbm, cand_ref)
    middle = len(copies)

    def normed(group):
        at = group * GROUP
        normed_ref[group * rows : (group + 1) * rows, :] = normed_rows(
            states_ref[at : at + GROUP],
            live_at[...],
            at,
            transform_ref[...],
            bias_ref[...],
            gain_ref[...],
            shift_ref[...],
        )

    for copy in copies[:early]:
        copy.wait()

    @pl.when(always)
    def _():
        place_of(rows, live_at, tokens_ref)
        normed(0)

    for copy in copies[early:middle]:
        copy.wait()
    bring(decoder_hbm.at[:, pl.ds(chunk, chunk)], next_ref)

    @pl.when(always)
    def _():
        for group in range(groups):
            if group + 1 < groups:
                normed(group + 1)
            part = normed_ref[group * rows : (group + 1) * rows, :]
            pool(part, decoder_ref, decoder_bias_ref[0], group, length, pooled)
        out_ref[:, :chunk] = keep_vocab(start_ref[0], pooled)
        depth = cand_ref.shape[0]
        wide = jnp.concatenate([cand_ref[...].astype(F32), jnp.zeros((depth, LANES - queries), F32)], axis=1)
        if depth < queries:
            wide = jnp.concatenate([wide, jnp.zeros((queries - depth, LANES), F32)], axis=0)
        out_ref[:, chunk:] = wide.astype(BF16)

    copies[-1].wait()


def chunk_kernel(at, last, start_ref, normed_ref, decoder_ref, decoder_bias_ref, *refs):
    if last:
        out_ref, pooled = refs
    else:
        far_ref, out_ref, next_ref, pooled, sem = refs
    queries, chunk = pooled.shape
    rows = normed_ref.shape[0] * GROUP // queries
    if not last:
        copy = pltpu.make_async_copy(far_ref.at[:, pl.ds((at + 1) * chunk, chunk)], next_ref, sem)
        copy.start()

    @pl.when(start_ref[0] >= 0)
    def _():
        for group in range(queries // GROUP):
            part = normed_ref[group * rows : (group + 1) * rows, :]
            pool(part, decoder_ref, decoder_bias_ref[at], group, rows // GROUP, pooled)
        out_ref[...] = keep_vocab(start_ref[0] + at * chunk, pooled)

    if not last:
        copy.wait()


def slot_queries(cand, base, tile_total):
    depth, queries = cand.shape
    row = lax.broadcasted_iota(jnp.int32, (tile_total, queries), 0) + base
    hits = jnp.zeros((tile_total, queries), F32)
    for place in range(depth):
        hits = jnp.where(cand[place : place + 1, :] == row, 1.0, hits)
    hits = hits.astype(BF16)
    mine = lax.broadcasted_iota(jnp.int32, (queries, queries), 0)
    other = lax.broadcasted_iota(jnp.int32, (queries, queries), 1)
    last = (((1,), (1,)), ((), ()))
    turned = lax.dot_general(
        jnp.where(mine == other, 1.0, 0.0).astype(BF16), hits, last, preferred_element_type=F32
    )
    before = lax.dot_general(
        jnp.where(other < mine, 1.0, 0.0).astype(BF16), hits, last, preferred_element_type=F32
    )
    rank = jnp.where(turned > 0.0, before, -1.0).astype(BF16)
    slots = tile_total * MOST
    tile = lax.broadcasted_iota(jnp.int32, (tile_total, slots), 0)
    spread = jnp.where(lax.broadcasted_iota(jnp.int32, (tile_total, slots), 1) // MOST == tile, 1.0, 0.0)
    wide = jnp.dot(rank, spread.astype(BF16), preferred_element_type=F32)
    want = (lax.broadcasted_iota(jnp.int32, (queries, slots), 1) % MOST).astype(F32)
    query = lax.broadcasted_iota(jnp.int32, (queries, slots), 0)
    return jnp.sum(jnp.where(wide == want, query, 0), axis=0, keepdims=True)


def score_kernel(at, last, parties, depth, place_ref, occupancy_ref, *refs):
    refs = list(refs)
    docs_ref = refs.pop(0) if at else None
    far_ref = None if last else refs.pop(0)
    weight_refs, refs = refs[:parties], refs[parties:]
    before_ref = refs.pop(0) if at else None
    if last:
        slots_ref, out_ref, turned, total = refs
    elif at:
        after_ref, next_ref, turned, sems = refs
    else:
        after_ref, next_ref, slots_ref, turned, sems, docs_ref, own_sems = refs
    tile_total, blocks, docs, terms = docs_ref.shape
    tiles = LANES // MOST
    steps = tile_total // tiles
    chunk = blocks * terms
    queries = weight_refs[0].shape[0]
    rows = tiles * docs
    always = place_ref[0] >= 0

    def fetch(part, target, signals):
        return [
            pltpu.make_async_copy(far_ref.at[tile, pl.ds(part * blocks, blocks)], target.at[tile], signals.at[tile])
            for tile in range(tile_total)
        ]

    own = [] if at else fetch(0, docs_ref, own_sems)
    later = [] if last else fetch(at + 1, next_ref, sems)
    queue = own + later

    def start(number):
        for copy in queue[:number]:
            copy.start()
        del queue[:number]

    start(2 * tiles if own else len(queue))

    @pl.when(always)
    def _():
        for party, ref in enumerate(weight_refs):
            turned[party * queries : (party + 1) * queries, :] = ref[:, :chunk]
            if not at:
                cand = ref[:depth, chunk : chunk + queries].astype(F32).astype(jnp.int32)
                found = slot_queries(cand, place_ref[0] * tile_total, tile_total)
                slots_ref[party : party + 1, :] = found + party * queries % LANES

    def work(step):
        left = [
            jnp.concatenate(
                [
                    jnp.where(
                        occupancy_ref[tile, at * blocks + block] != 0, docs_ref[tile, block], 0.0
                    ).astype(BF16)
                    for block in range(blocks)
                ],
                axis=1,
            )
            for tile in range(step * tiles, (step + 1) * tiles)
        ]
        value = lax.dot_general(
            jnp.concatenate(left, axis=0),
            turned[...],
            (((1,), (1,)), ((), ())),
            preferred_element_type=F32,
        )
        if at:
            value = value + before_ref[step * rows : (step + 1) * rows, :]
        if not last:
            after_ref[step * rows : (step + 1) * rows, :] = value
            return
        lane = lax.broadcasted_iota(jnp.int32, (docs, LANES), 1) // MOST
        term_count, share = total.shape[1], docs // total.shape[1]
        for party in range(parties):
            begin = party * queries // LANES * LANES
            source = slots_ref[party : party + 1, step * LANES : (step + 1) * LANES]
            source = jnp.broadcast_to(source, (docs, LANES))
            part = None
            for tile in range(tiles):
                held = value[tile * docs : (tile + 1) * docs, begin : begin + LANES]
                held = jnp.take_along_axis(held, source, axis=1, mode="promise_in_bounds")
                part = held if part is None else jnp.where(lane == tile, held, part)
            for term in range(term_count):
                total[party, term, step * share : (step + 1) * share, :] = part[term * share : (term + 1) * share]

    if own:
        for step in range(steps):
            for copy in own[step * tiles : (step + 1) * tiles]:
                copy.wait()
            start(2 * tiles)

            @pl.when(always)
            def _(step=step):
                work(step)
    else:

        @pl.when(always)
        def _():
            for step in range(steps):
                work(step)
            if last:
                for party in range(parties):
                    out_ref[place_ref[0] ^ party] = total[party].astype(BF16)

    start(len(queue))
    for copy in later:
        copy.wait()


def ranks(cand, row, queries):
    depth, total = cand.shape
    hits = jnp.zeros((row.shape[0], total), F32)
    for place in range(depth):
        hits = jnp.where(cand[place : place + 1, :] == row, 1.0, hits)
    earlier = lax.broadcasted_iota(jnp.int32, (total, total), 0)
    later = lax.broadcasted_iota(jnp.int32, (total, total), 1)
    before = jnp.dot(
        hits.astype(BF16), jnp.where(earlier < later, 1.0, 0.0).astype(BF16), preferred_element_type=F32
    )
    return jnp.where(hits > 0.0, before, -1.0)


def final_kernel(cand_ref, got_ref, out_ref):
    docs_n, term_count, rows, _ = got_ref.shape
    depth, share, queries = out_ref.shape
    groups = rows // share
    tiles = LANES // MOST
    all_tiles = docs_n * groups * tiles
    cand = cand_ref[...]
    rank = ranks(cand, lax.broadcasted_iota(jnp.int32, (all_tiles, queries), 0), queries)
    slot = lax.broadcasted_iota(jnp.int32, (LANES, tiles * queries), 0)
    twice = jnp.concatenate([cand, cand], axis=1)
    lane = lax.broadcasted_iota(jnp.int32, (1, 2 * queries), 1) // queries
    result = [jnp.zeros((share, 2 * queries), F32) for _ in range(depth)]
    for doc in range(docs_n):
        summed = got_ref[doc, 0].astype(F32)
        for term in range(1, term_count):
            summed = summed + got_ref[doc, term].astype(F32)
        for group in range(groups):
            first = (doc * groups + group) * tiles
            want = jnp.concatenate(
                [
                    jnp.where(rank[first + k : first + k + 1] >= 0.0, rank[first + k : first + k + 1] + k * MOST, -1.0)
                    for k in range(tiles)
                ],
                axis=1,
            ).astype(jnp.int32)
            hot = jnp.where(slot == want, 1.0, 0.0).astype(BF16)
            value = summed[group * share : (group + 1) * share]
            high = value.astype(BF16)
            low = (value - high.astype(F32)).astype(BF16)
            moved = jnp.dot(high, hot, preferred_element_type=F32) + jnp.dot(
                low, hot, preferred_element_type=F32
            )
            for pair in range(tiles // 2):
                held = moved[:, pair * 2 * queries : (pair + 1) * 2 * queries]
                name = first + pair * 2 + lane
                for place in range(depth):
                    result[place] = jnp.where(twice[place : place + 1] == name, held, result[place])
    for place in range(depth):
        out_ref[place] = result[place][:, :queries] + result[place][:, queries:]


def body(
    query_states,
    token_ids,
    transform_weight,
    transform_bias,
    norm_gain,
    norm_bias,
    decoder_weight,
    decoder_bias,
    candidates,
    occupancy,
    doc_blocks,
):
    query_count, length, width = query_states.shape
    vocab = decoder_weight.shape[1]
    tile_local, blocks, docs, terms = doc_blocks.shape
    depth = candidates.shape[1]
    term_index, doc_index = lax.axis_index("term"), lax.axis_index("doc")
    doc_count, term_count = lax.axis_size("doc"), lax.axis_size("term")
    share = docs // term_count
    all_queries = doc_count * query_count
    tiles = LANES // MOST
    steps = tile_local // tiles
    chunks = 3
    chunk = vocab // chunks
    few = blocks // chunks
    cand = candidates.T
    start = (term_index * vocab).reshape(1)
    place = doc_index.reshape(1)
    rows = query_count * length
    far, near = pltpu.HBM, pltpu.VMEM

    def put(space, *operands):
        return [pltpu.with_memory_space_constraint(operand, space) for operand in operands]

    def call(name, kernel, in_specs, out_shape, scratch, macs, limit, operands):
        return pl.pallas_call(
            kernel,
            in_specs=in_specs,
            out_specs=jax.tree.map(lambda _: WHOLE, out_shape),
            out_shape=out_shape,
            scratch_shapes=scratch,
            cost_estimate=pl.CostEstimate(flops=2 * macs, bytes_accessed=10**6, transcendentals=0),
            compiler_params=pltpu.CompilerParams(vmem_limit_bytes=limit),
            name=name,
        )(*operands)

    next_decoder = near((width, chunk), BF16)
    next_docs = near((tile_local, few, docs, terms), BF16)
    pooled = pltpu.VMEM((query_count, chunk), F32)
    piece, normed, first_decoder, all_bias = call(
        "expand_first",
        first_kernel,
        [SCALARS] + [FAR] * 9,
        [
            jax.ShapeDtypeStruct((query_count, chunk + LANES), BF16),
            near((rows, width), BF16),
            next_decoder,
            near((chunks, 1, chunk), F32),
        ],
        [
            pltpu.VMEM(query_states.shape, BF16),
            pltpu.VMEM(transform_weight.shape, BF16),
            pltpu.VMEM((width, chunk), BF16),
            pltpu.VMEM((1, width), F32),
            pltpu.VMEM((1, width), F32),
            pltpu.VMEM((1, width), F32),
            pltpu.VMEM((length, query_count), jnp.int32),
            pltpu.VMEM(cand.shape, jnp.int32),
            pltpu.VMEM((GROUP * length, query_count), F32),
            pooled,
            pltpu.SemaphoreType.DMA((10 + chunks,)),
        ],
        rows * width * (width + chunk),
        13 << 20,
        [start]
        + put(
            far,
            query_states,
            token_ids.T,
            transform_weight,
            transform_bias,
            norm_gain,
            norm_bias,
            decoder_weight,
            decoder_bias,
            cand,
        ),
    )
    own, decoder = [piece], [first_decoder]
    for at in range(1, chunks):
        final = at == chunks - 1
        piece, *decoder = call(
            "expand_next",
            functools.partial(chunk_kernel, at, final),
            [SCALARS] + [WHOLE] * 3 + ([] if final else [FAR]),
            [jax.ShapeDtypeStruct((query_count, chunk), BF16)] + ([] if final else [next_decoder]),
            [pooled] + ([] if final else [pltpu.SemaphoreType.DMA(())]),
            rows * width * chunk,
            6 << 20,
            [start, *put(near, normed, *decoder, all_bias), *([] if final else put(far, decoder_weight))],
        )
        own.append(piece)

    partial_scores, slots = None, None
    for at in range(chunks):
        held = [own[at]] + [None] * (doc_count - 1)
        bit, known = doc_count // 2, [0]
        while bit:
            swap = [(i, i ^ bit) for i in range(doc_count)]
            for k in list(known):
                held[k | bit] = lax.ppermute(held[k], "doc", swap)
                known.append(k | bit)
            if at >= 2 and bit == doc_count // 2:
                held[bit], partial_scores = lax.optimization_barrier((held[bit], partial_scores))
            bit //= 2
        last = at == chunks - 1
        if last:
            out_shape = [jax.ShapeDtypeStruct((doc_count, term_count, steps * share, LANES), BF16)]
            scratch = [pltpu.VMEM((doc_count, term_count, steps * share, LANES), F32)]
        else:
            out_shape = [near((tile_local * docs, all_queries), F32), next_docs]
            if at == 0:
                out_shape.append(near((doc_count, tile_local * MOST), jnp.int32))
            scratch = [pltpu.SemaphoreType.DMA((tile_local,))]
            if at == 0:
                scratch += [
                    pltpu.VMEM((tile_local, few, docs, terms), BF16),
                    pltpu.SemaphoreType.DMA((tile_local,)),
                ]
        operands = [place, occupancy, *(put(near, near_docs) if at else [])]
        in_specs = [SCALARS, SCALARS] + [WHOLE] * min(at, 1)
        if not last:
            operands += put(far, doc_blocks)
            in_specs.append(FAR)
        extra = ([partial_scores] if at else []) + ([slots] if last else [])
        operands += held + put(near, *extra)
        in_specs += [WHOLE] * (doc_count + len(extra))
        results = call(
            "score_last" if last else "score_chunk",
            functools.partial(score_kernel, at, last, doc_count, depth),
            in_specs,
            out_shape,
            [pltpu.VMEM((all_queries, chunk), BF16)] + scratch,
            4 * tile_local * docs * chunk * all_queries,
            (8 if at else 14) << 20,
            operands,
        )
        if last:
            sent = results[0]
        else:
            partial_scores, near_docs = results[:2]
            slots = results[2] if at == 0 else slots
    weights = jnp.concatenate([own[0][:, :chunk], *own[1:]], axis=1)

    everyone = doc_count * term_count
    got = lax.all_to_all(
        sent.reshape(everyone, steps * share, LANES), ("doc", "term"), split_axis=0, concat_axis=0, tiled=True
    ).reshape(doc_count, term_count, steps * share, LANES)
    scores = call(
        "place",
        final_kernel,
        [WHOLE, WHOLE],
        jax.ShapeDtypeStruct((depth, share, query_count), F32),
        [],
        10**6,
        8 << 20,
        [cand, got],
    )
    return weights, scores.transpose(2, 0, 1)


def solution(mesh):
    placed = (
        P("doc", None, None),
        P("doc", None),
        P(),
        P(),
        P(),
        P(),
        P(None, "term"),
        P("term"),
        P("doc", None),
        P("doc", "term"),
        P("doc", "term", None, None),
    )
    return jax.shard_map(
        body,
        mesh=mesh,
        in_specs=placed,
        out_specs=(P("doc", "term"), P("doc", None, "term")),
        check_vma=False,
    )
```

```python
import functools
import math

import jax
import jax.numpy as jnp
from jax import lax
from jax.experimental import pallas as pl
from jax.experimental.pallas import tpu as pltpu
from jax.sharding import PartitionSpec as P

VOCAB = 30522
MOST = 32
LANES = 128
GROUP = 8
F32 = jnp.float32
BF16 = jnp.bfloat16
WHOLE = pl.BlockSpec(memory_space=pltpu.VMEM)
FAR = pl.BlockSpec(memory_space=pltpu.HBM)
SCALARS = pl.BlockSpec(memory_space=pltpu.SMEM)


def gelu(value):
    return 0.5 * value * (1.0 + lax.erf(value * math.sqrt(0.5)))


def normed_rows(states, live_at, first, transform, bias, gain, shift):
    queries, length, width = states.shape
    rows = queries * length
    row = lax.broadcasted_iota(jnp.int32, live_at.shape, 0)
    lane = lax.broadcasted_iota(jnp.int32, live_at.shape, 1)
    own = jnp.where(lane == first + row % queries, live_at, 0.0)
    live = jnp.sum(own, axis=1, keepdims=True) > 0.0
    row = lax.broadcasted_iota(jnp.int32, (rows, 1), 0)
    source = row % queries * length + jnp.where(live, row // queries, 0)
    column = lax.broadcasted_iota(jnp.int32, (rows, rows), 1)
    order = jnp.where(column == source, 1.0, 0.0).astype(BF16)
    moved = jnp.dot(order, states.reshape(rows, width), preferred_element_type=F32)
    hidden = jnp.dot(moved.astype(BF16), transform, preferred_element_type=F32)
    hidden = gelu(hidden + bias)
    centred = hidden - jnp.mean(hidden, axis=1, keepdims=True)
    spread = jnp.mean(centred * centred, axis=1, keepdims=True)
    return (centred * lax.rsqrt(spread + 1e-06) * gain + shift).astype(BF16)


def place_of(rows, live_at, tokens_ref):
    length = tokens_ref.shape[0]
    at = lax.broadcasted_iota(jnp.int32, (rows, length), 0) // GROUP
    spot = lax.broadcasted_iota(jnp.int32, (rows, length), 1)
    pick = jnp.where(at == spot, 1.0, 0.0).astype(BF16)
    alive = jnp.where(tokens_ref[...] != 0, 1.0, 0.0).astype(BF16)
    live_at[...] = jnp.dot(pick, alive, preferred_element_type=F32)


def pool(rows, decoder_ref, bias, group, length, out_ref):
    logits = jnp.dot(rows, decoder_ref[...], preferred_element_type=F32)
    top = jnp.max(logits.reshape(length, GROUP, logits.shape[1]), axis=0)
    out_ref[group * GROUP : (group + 1) * GROUP, :] = jnp.log1p(
        jnp.maximum(top + bias, 0.0)
    )


def keep_vocab(start, pooled):
    column = start + lax.broadcasted_iota(jnp.int32, pooled.shape, 1)
    return jnp.where(column < VOCAB, pooled[...], 0.0).astype(BF16)


def first_kernel(
    start_ref,
    states_hbm,
    tokens_hbm,
    transform_hbm,
    bias_hbm,
    gain_hbm,
    shift_hbm,
    decoder_hbm,
    decoder_bias_hbm,
    cand_hbm,
    out_ref,
    normed_ref,
    next_ref,
    decoder_bias_ref,
    states_ref,
    transform_ref,
    decoder_ref,
    bias_ref,
    gain_ref,
    shift_ref,
    tokens_ref,
    cand_ref,
    live_at,
    pooled,
    sems,
):
    queries, length, _ = states_ref.shape
    groups = queries // GROUP
    rows = GROUP * length
    chunk = decoder_ref.shape[1]
    always = start_ref[0] >= 0
    copies = []

    def bring(source, target):
        copy = pltpu.make_async_copy(source, target, sems.at[len(copies)])
        copies.append(copy)
        copy.start()

    half = pl.ds(0, GROUP)
    other = pl.ds(GROUP, queries - GROUP)
    bring(tokens_hbm, tokens_ref)
    bring(bias_hbm, bias_ref.at[0])
    bring(gain_hbm, gain_ref.at[0])
    bring(shift_hbm, shift_ref.at[0])
    bring(states_hbm.at[half], states_ref.at[half])
    bring(transform_hbm, transform_ref)
    early = len(copies)
    bring(decoder_hbm.at[:, pl.ds(0, chunk)], decoder_ref)
    bring(decoder_bias_hbm, decoder_bias_ref.at[0])
    bring(states_hbm.at[other], states_ref.at[other])
    bring(cand_hbm, cand_ref)
    middle = len(copies)

    def normed(group):
        at = group * GROUP
        normed_ref[group * rows : (group + 1) * rows, :] = normed_rows(
            states_ref[at : at + GROUP],
            live_at[...],
            at,
            transform_ref[...],
            bias_ref[...],
            gain_ref[...],
            shift_ref[...],
        )

    for copy in copies[:early]:
        copy.wait()

    @pl.when(always)
    def _():
        place_of(rows, live_at, tokens_ref)
        normed(0)

    for copy in copies[early:middle]:
        copy.wait()
    bring(decoder_hbm.at[:, pl.ds(chunk, next_ref.shape[1])], next_ref)

    @pl.when(always)
    def _():
        for group in range(groups):
            if group + 1 < groups:
                normed(group + 1)
            part = normed_ref[group * rows : (group + 1) * rows, :]
            pool(part, decoder_ref, decoder_bias_ref[:, :chunk], group, length, pooled)
        out_ref[:, :chunk] = keep_vocab(start_ref[0], pooled)
        depth = cand_ref.shape[0]
        wide = jnp.concatenate([cand_ref[...].astype(F32), jnp.zeros((depth, LANES - queries), F32)], axis=1)
        if depth < queries:
            wide = jnp.concatenate([wide, jnp.zeros((queries - depth, LANES), F32)], axis=0)
        out_ref[:, chunk:] = wide.astype(BF16)

    copies[-1].wait()


def chunk_kernel(begin, start_ref, normed_ref, decoder_ref, decoder_bias_ref, out_ref, pooled):
    queries, chunk = pooled.shape
    rows = normed_ref.shape[0] * GROUP // queries
    for group in range(queries // GROUP):
        part = normed_ref[group * rows : (group + 1) * rows, :]
        bias = decoder_bias_ref[:, begin : begin + chunk]
        pool(part, decoder_ref, bias, group, rows // GROUP, pooled)
    out_ref[...] = keep_vocab(start_ref[0] + begin, pooled)


def middle_kernel(
    begin, start_ref, normed_ref, decoder_ref, decoder_bias_ref, far_ref, out_ref, next_ref, pooled, sem
):
    last = begin + pooled.shape[1]
    copy = pltpu.make_async_copy(far_ref.at[:, pl.ds(last, next_ref.shape[1])], next_ref, sem)
    copy.start()

    @pl.when(start_ref[0] >= 0)
    def _():
        chunk_kernel(begin, start_ref, normed_ref, decoder_ref, decoder_bias_ref, out_ref, pooled)

    copy.wait()


def slot_queries(cand, base, tile_total):
    depth, queries = cand.shape
    row = lax.broadcasted_iota(jnp.int32, (tile_total, queries), 0) + base
    hits = jnp.zeros((tile_total, queries), F32)
    for place in range(depth):
        hits = jnp.where(cand[place : place + 1, :] == row, 1.0, hits)
    hits = hits.astype(BF16)
    mine = lax.broadcasted_iota(jnp.int32, (queries, queries), 0)
    other = lax.broadcasted_iota(jnp.int32, (queries, queries), 1)
    last = (((1,), (1,)), ((), ()))
    turned = lax.dot_general(
        jnp.where(mine == other, 1.0, 0.0).astype(BF16), hits, last, preferred_element_type=F32
    )
    before = lax.dot_general(
        jnp.where(other < mine, 1.0, 0.0).astype(BF16), hits, last, preferred_element_type=F32
    )
    rank = jnp.where(turned > 0.0, before, -1.0).astype(BF16)
    slots = tile_total * MOST
    tile = lax.broadcasted_iota(jnp.int32, (tile_total, slots), 0)
    spread = jnp.where(lax.broadcasted_iota(jnp.int32, (tile_total, slots), 1) // MOST == tile, 1.0, 0.0)
    wide = jnp.dot(rank, spread.astype(BF16), preferred_element_type=F32)
    want = (lax.broadcasted_iota(jnp.int32, (queries, slots), 1) % MOST).astype(F32)
    query = lax.broadcasted_iota(jnp.int32, (queries, slots), 0)
    return jnp.sum(jnp.where(wide == want, query, 0), axis=0, keepdims=True)


def docs_copies(far_ref, begin, target, sems):
    tile_total, blocks, _, _ = target.shape
    part = pl.ds(begin, blocks)
    return [
        pltpu.make_async_copy(far_ref.at[tile, part], target.at[tile], sems.at[tile]) for tile in range(tile_total)
    ]


def gather_weights(weight_refs, turned):
    queries = weight_refs[0].shape[0]
    for party, ref in enumerate(weight_refs):
        turned[party * queries : (party + 1) * queries, :] = ref[:, : turned.shape[1]]


def step_scores(step, begin, occupancy_ref, docs_ref, turned):
    tiles = LANES // MOST
    left = [
        jnp.concatenate(
            [
                jnp.where(occupancy_ref[tile, begin + block] != 0, docs_ref[tile, block], 0.0).astype(BF16)
                for block in range(docs_ref.shape[1])
            ],
            axis=1,
        )
        for tile in range(step * tiles, (step + 1) * tiles)
    ]
    return lax.dot_general(
        jnp.concatenate(left, axis=0), turned[...], (((1,), (1,)), ((), ())), preferred_element_type=F32
    )


def first_score_kernel(parties, depth, place_ref, occupancy_ref, far_ref, *refs):
    weight_refs = refs[:parties]
    after_ref, next_ref, slots_ref, turned, docs_ref, own_sems, next_sems = refs[parties:]
    tile_total, blocks, docs, _ = docs_ref.shape
    tiles = LANES // MOST
    rows = tiles * docs
    queries, chunk = weight_refs[0].shape[0], turned.shape[1]
    always = place_ref[0] >= 0
    own = docs_copies(far_ref, 0, docs_ref, own_sems)
    later = docs_copies(far_ref, blocks, next_ref, next_sems)
    queue = own + later

    def start(number):
        for copy in queue[:number]:
            copy.start()
        del queue[:number]

    start(3 * tiles)

    @pl.when(always)
    def _():
        gather_weights(weight_refs, turned)
        for party, ref in enumerate(weight_refs):
            cand = ref[:depth, chunk : chunk + queries].astype(F32).astype(jnp.int32)
            found = slot_queries(cand, place_ref[0] * tile_total, tile_total)
            slots_ref[party : party + 1, :] = found + party * queries % LANES

    start(2 * tiles)
    for step in range(tile_total // tiles):
        for copy in own[step * tiles : (step + 1) * tiles]:
            copy.wait()
        start(2 * tiles)

        @pl.when(always)
        def _(step=step):
            after_ref[step * rows : (step + 1) * rows, :] = step_scores(step, 0, occupancy_ref, docs_ref, turned)

    start(len(queue))
    for copy in later:
        copy.wait()


def middle_score_kernel(begin, parties, place_ref, occupancy_ref, docs_ref, before_ref, far_ref, *refs):
    weight_refs = refs[:parties]
    after_ref, next_ref, turned, sems = refs[parties:]
    tile_total, blocks, docs, _ = docs_ref.shape
    rows = LANES // MOST * docs
    copies = docs_copies(far_ref, begin + blocks, next_ref, sems)
    for copy in copies:
        copy.start()

    @pl.when(place_ref[0] >= 0)
    def _():
        gather_weights(weight_refs, turned)
        for step in range(tile_total * docs // rows):
            part = slice(step * rows, (step + 1) * rows)
            after_ref[part, :] = before_ref[part, :] + step_scores(step, begin, occupancy_ref, docs_ref, turned)

    for copy in copies:
        copy.wait()


def last_score_kernel(begin, parties, place_ref, occupancy_ref, docs_ref, before_ref, slots_ref, *refs):
    weight_refs = refs[:parties]
    out_ref, turned, total = refs[parties:]
    tile_total, _, docs, _ = docs_ref.shape
    tiles = LANES // MOST
    rows = tiles * docs
    queries = weight_refs[0].shape[0]
    term_count, share = total.shape[1], docs // total.shape[1]
    gather_weights(weight_refs, turned)
    lane = lax.broadcasted_iota(jnp.int32, (docs, LANES), 1) // MOST
    for step in range(tile_total // tiles):
        value = before_ref[step * rows : (step + 1) * rows, :]
        value = value + step_scores(step, begin, occupancy_ref, docs_ref, turned)
        for party in range(parties):
            column = party * queries // LANES * LANES
            source = slots_ref[party : party + 1, step * LANES : (step + 1) * LANES]
            source = jnp.broadcast_to(source, (docs, LANES))
            part = None
            for tile in range(tiles):
                held = value[tile * docs : (tile + 1) * docs, column : column + LANES]
                held = jnp.take_along_axis(held, source, axis=1, mode="promise_in_bounds")
                part = held if part is None else jnp.where(lane == tile, held, part)
            for term in range(term_count):
                total[party, term, step * share : (step + 1) * share, :] = part[term * share : (term + 1) * share]
    for party in range(parties):
        out_ref[place_ref[0] ^ party] = total[party].astype(BF16)


def ranks(cand, row, queries):
    depth, total = cand.shape
    hits = jnp.zeros((row.shape[0], total), F32)
    for place in range(depth):
        hits = jnp.where(cand[place : place + 1, :] == row, 1.0, hits)
    earlier = lax.broadcasted_iota(jnp.int32, (total, total), 0)
    later = lax.broadcasted_iota(jnp.int32, (total, total), 1)
    before = jnp.dot(
        hits.astype(BF16), jnp.where(earlier < later, 1.0, 0.0).astype(BF16), preferred_element_type=F32
    )
    return jnp.where(hits > 0.0, before, -1.0)


def choice_kernel(cand_ref, out_ref):
    queries = cand_ref.shape[1]
    groups = out_ref.shape[0]
    tiles = LANES // MOST
    cand = cand_ref[...]
    rank = ranks(cand, lax.broadcasted_iota(jnp.int32, (groups * tiles, queries), 0), queries)
    slot = lax.broadcasted_iota(jnp.int32, (LANES, tiles * queries), 0)
    for group in range(groups):
        want = [rank[group * tiles + k : group * tiles + k + 1] for k in range(tiles)]
        want = [jnp.where(w >= 0.0, w + k * MOST, -1.0) for k, w in enumerate(want)]
        want = jnp.concatenate(want, axis=1).astype(jnp.int32)
        out_ref[group] = jnp.where(slot == want, 1.0, 0.0).astype(BF16)


def final_kernel(cand_ref, choice_ref, got_ref, out_ref):
    docs_n, term_count, rows, _ = got_ref.shape
    depth, share, queries = out_ref.shape
    groups = rows // share
    tiles = LANES // MOST
    cand = cand_ref[...]
    twice = jnp.concatenate([cand, cand], axis=1)
    lane = lax.broadcasted_iota(jnp.int32, (1, 2 * queries), 1) // queries
    result = [jnp.zeros((share, 2 * queries), F32) for _ in range(depth)]
    for doc in range(docs_n):
        summed = got_ref[doc, 0].astype(F32)
        for term in range(1, term_count):
            summed = summed + got_ref[doc, term].astype(F32)
        for group in range(groups):
            first = (doc * groups + group) * tiles
            value = summed[group * share : (group + 1) * share]
            high = value.astype(BF16)
            low = (value - high.astype(F32)).astype(BF16)
            both = jnp.concatenate([high, low], axis=0)
            moved = jnp.dot(both, choice_ref[doc * groups + group], preferred_element_type=F32)
            moved = moved[:share] + moved[share:]
            for pair in range(tiles // 2):
                held = moved[:, pair * 2 * queries : (pair + 1) * 2 * queries]
                name = first + pair * 2 + lane
                for place in range(depth):
                    result[place] = jnp.where(twice[place : place + 1] == name, held, result[place])
    for place in range(depth):
        out_ref[place] = result[place][:, :queries] + result[place][:, queries:]


def body(
    query_states,
    token_ids,
    transform_weight,
    transform_bias,
    norm_gain,
    norm_bias,
    decoder_weight,
    decoder_bias,
    candidates,
    occupancy,
    doc_blocks,
):
    query_count, length, width = query_states.shape
    vocab = decoder_weight.shape[1]
    tile_local, blocks, docs, terms = doc_blocks.shape
    depth = candidates.shape[1]
    term_index, doc_index = lax.axis_index("term"), lax.axis_index("doc")
    doc_count, term_count = lax.axis_size("doc"), lax.axis_size("term")
    share = docs // term_count
    all_queries = doc_count * query_count
    tiles = LANES // MOST
    steps = tile_local // tiles
    cuts = (0, blocks // 3, blocks * 11 // 15, blocks)
    few = [cuts[k + 1] - cuts[k] for k in range(3)]
    chunks = [count * terms for count in few]
    begins = [cut * terms for cut in cuts[:3]]
    cand = candidates.T
    start = (term_index * vocab).reshape(1)
    place = doc_index.reshape(1)
    rows = query_count * length
    far, near = pltpu.HBM, pltpu.VMEM

    def put(space, *operands):
        return [pltpu.with_memory_space_constraint(operand, space) for operand in operands]

    def call(name, kernel, in_specs, out_shape, scratch, macs, limit, operands):
        return pl.pallas_call(
            kernel,
            in_specs=in_specs,
            out_specs=jax.tree.map(lambda _: WHOLE, out_shape),
            out_shape=out_shape,
            scratch_shapes=scratch,
            cost_estimate=pl.CostEstimate(flops=2 * macs, bytes_accessed=10**6, transcendentals=0),
            compiler_params=pltpu.CompilerParams(vmem_limit_bytes=limit),
            name=name,
        )(*operands)

    def next_docs(at):
        return near((tile_local, few[at], docs, terms), BF16)

    def pooled(at):
        return pltpu.VMEM((query_count, chunks[at]), F32)

    def turned(at):
        return pltpu.VMEM((all_queries, chunks[at]), BF16)

    def piece(at):
        return jax.ShapeDtypeStruct((query_count, chunks[at]), BF16)

    signals = pltpu.SemaphoreType.DMA((tile_local,))
    running = near((tile_local * docs, all_queries), F32)
    expand_macs = [rows * width * chunk for chunk in chunks]
    score_macs = [4 * tile_local * docs * chunk * all_queries for chunk in chunks]
    xor = [[(i, i ^ k) for i in range(doc_count)] for k in range(doc_count)]

    def spread(own, after):
        held = [own] + [None] * (doc_count - 1)
        bit, known = doc_count // 2, [0]
        while bit:
            for k in list(known):
                held[k | bit] = lax.ppermute(held[k], "doc", xor[bit])
                known.append(k | bit)
            if bit == doc_count // 2:
                held[bit], _ = lax.optimization_barrier((held[bit], after))
            bit //= 2
        return held

    first, normed, decoder, all_bias = call(
        "expand_first",
        first_kernel,
        [SCALARS] + [FAR] * 9,
        [
            jax.ShapeDtypeStruct((query_count, chunks[0] + LANES), BF16),
            near((rows, width), BF16),
            near((width, chunks[1]), BF16),
            near((1, vocab), F32),
        ],
        [
            pltpu.VMEM(query_states.shape, BF16),
            pltpu.VMEM(transform_weight.shape, BF16),
            pltpu.VMEM((width, chunks[0]), BF16),
            pltpu.VMEM((1, width), F32),
            pltpu.VMEM((1, width), F32),
            pltpu.VMEM((1, width), F32),
            pltpu.VMEM((length, query_count), jnp.int32),
            pltpu.VMEM(cand.shape, jnp.int32),
            pltpu.VMEM((GROUP * length, query_count), F32),
            pooled(0),
            pltpu.SemaphoreType.DMA((11,)),
        ],
        rows * width * width + expand_macs[0],
        13 << 20,
        [start]
        + put(
            far,
            query_states,
            token_ids.T,
            transform_weight,
            transform_bias,
            norm_gain,
            norm_bias,
            decoder_weight,
            decoder_bias,
            cand,
        ),
    )
    middle, decoder = call(
        "expand_middle",
        functools.partial(middle_kernel, begins[1]),
        [SCALARS] + [WHOLE] * 3 + [FAR],
        [piece(1), near((width, chunks[2]), BF16)],
        [pooled(1), pltpu.SemaphoreType.DMA(())],
        expand_macs[1],
        7 << 20,
        [start, *put(near, normed, decoder, all_bias), *put(far, decoder_weight)],
    )
    first_all = spread(first, middle)
    last = call(
        "expand_last",
        functools.partial(chunk_kernel, begins[2]),
        [SCALARS] + [WHOLE] * 3,
        piece(2),
        [pooled(2)],
        expand_macs[2],
        7 << 20,
        [start, *put(near, normed, decoder, all_bias)],
    )
    scores, near_docs, slots = call(
        "score_first",
        functools.partial(first_score_kernel, doc_count, depth),
        [SCALARS] * 2 + [FAR] + [WHOLE] * doc_count,
        [running, next_docs(1), near((doc_count, tile_local * MOST), jnp.int32)],
        [turned(0), pltpu.VMEM((tile_local, few[0], docs, terms), BF16), signals, signals],
        score_macs[0],
        14 << 20,
        [place, occupancy, *put(far, doc_blocks), *first_all],
    )
    last_all = spread(last, scores)
    middle_all = spread(middle, last)
    scores, near_docs = call(
        "score_middle",
        functools.partial(middle_score_kernel, cuts[1], doc_count),
        [SCALARS] * 2 + [WHOLE] * 2 + [FAR] + [WHOLE] * doc_count,
        [running, next_docs(2)],
        [turned(1), signals],
        score_macs[1],
        8 << 20,
        [place, occupancy, *put(near, near_docs, scores), *put(far, doc_blocks), *middle_all],
    )
    sent = call(
        "score_last",
        functools.partial(last_score_kernel, cuts[2], doc_count),
        [SCALARS] * 2 + [WHOLE] * (3 + doc_count),
        jax.ShapeDtypeStruct((doc_count, term_count, steps * share, LANES), BF16),
        [turned(2), pltpu.VMEM((doc_count, term_count, steps * share, LANES), F32)],
        score_macs[2],
        8 << 20,
        [place, occupancy, *put(near, near_docs, scores, slots), *last_all],
    )
    weights = jnp.concatenate([first[:, : chunks[0]], middle, last], axis=1)

    everyone = doc_count * term_count
    got = lax.all_to_all(
        sent.reshape(everyone, steps * share, LANES), ("doc", "term"), split_axis=0, concat_axis=0, tiled=True
    ).reshape(doc_count, term_count, steps * share, LANES)
    choices = call(
        "choices",
        choice_kernel,
        [WHOLE],
        jax.ShapeDtypeStruct((doc_count * steps, LANES, tiles * query_count), BF16),
        [],
        10**6,
        8 << 20,
        [cand],
    )
    scores = call(
        "place",
        final_kernel,
        [WHOLE] * 3,
        jax.ShapeDtypeStruct((depth, share, query_count), F32),
        [],
        10**6,
        8 << 20,
        [cand, choices, got],
    )
    return weights, scores.transpose(2, 0, 1)


def solution(mesh):
    placed = (
        P("doc", None, None),
        P("doc", None),
        P(),
        P(),
        P(),
        P(),
        P(None, "term"),
        P("term"),
        P("doc", None),
        P("doc", "term"),
        P("doc", "term", None, None),
    )
    return jax.shard_map(
        body,
        mesh=mesh,
        in_specs=placed,
        out_specs=(P("doc", "term"), P("doc", None, "term")),
        check_vma=False,
    )
```

```python
import functools
import math

import jax
import jax.numpy as jnp
from jax import lax
from jax.experimental import pallas as pl
from jax.experimental.pallas import tpu as pltpu
from jax.sharding import PartitionSpec as P

VOCAB = 30522
MOST = 32
LANES = 128
GROUP = 8
F32 = jnp.float32
BF16 = jnp.bfloat16
WHOLE = pl.BlockSpec(memory_space=pltpu.VMEM)
FAR = pl.BlockSpec(memory_space=pltpu.HBM)
SCALARS = pl.BlockSpec(memory_space=pltpu.SMEM)


def gelu(value):
    return 0.5 * value * (1.0 + lax.erf(value * math.sqrt(0.5)))


def normed_rows(states, live_at, first, transform, bias, gain, shift):
    queries, length, width = states.shape
    rows = queries * length
    row = lax.broadcasted_iota(jnp.int32, live_at.shape, 0)
    lane = lax.broadcasted_iota(jnp.int32, live_at.shape, 1)
    own = jnp.where(lane == first + row % queries, live_at, 0.0)
    live = jnp.sum(own, axis=1, keepdims=True) > 0.0
    row = lax.broadcasted_iota(jnp.int32, (rows, 1), 0)
    source = row % queries * length + jnp.where(live, row // queries, 0)
    column = lax.broadcasted_iota(jnp.int32, (rows, rows), 1)
    order = jnp.where(column == source, 1.0, 0.0).astype(BF16)
    moved = jnp.dot(order, states.reshape(rows, width), preferred_element_type=F32)
    hidden = jnp.dot(moved.astype(BF16), transform, preferred_element_type=F32)
    hidden = gelu(hidden + bias)
    centred = hidden - jnp.mean(hidden, axis=1, keepdims=True)
    spread = jnp.mean(centred * centred, axis=1, keepdims=True)
    return (centred * lax.rsqrt(spread + 1e-06) * gain + shift).astype(BF16)


def place_of(rows, live_at, tokens_ref):
    length = tokens_ref.shape[0]
    at = lax.broadcasted_iota(jnp.int32, (rows, length), 0) // GROUP
    spot = lax.broadcasted_iota(jnp.int32, (rows, length), 1)
    pick = jnp.where(at == spot, 1.0, 0.0).astype(BF16)
    alive = jnp.where(tokens_ref[...] != 0, 1.0, 0.0).astype(BF16)
    live_at[...] = jnp.dot(pick, alive, preferred_element_type=F32)


def pool(rows, decoder_ref, bias, group, length, out_ref):
    logits = jnp.dot(rows, decoder_ref[...], preferred_element_type=F32)
    top = jnp.max(logits.reshape(length, GROUP, logits.shape[1]), axis=0)
    out_ref[group * GROUP : (group + 1) * GROUP, :] = jnp.log1p(
        jnp.maximum(top + bias, 0.0)
    )


def keep_vocab(start, pooled):
    column = start + lax.broadcasted_iota(jnp.int32, pooled.shape, 1)
    return jnp.where(column < VOCAB, pooled[...], 0.0).astype(BF16)


def first_kernel(
    start_ref,
    states_hbm,
    tokens_hbm,
    transform_hbm,
    bias_hbm,
    gain_hbm,
    shift_hbm,
    decoder_hbm,
    decoder_bias_hbm,
    cand_hbm,
    out_ref,
    normed_ref,
    next_ref,
    decoder_bias_ref,
    states_ref,
    transform_ref,
    decoder_ref,
    bias_ref,
    gain_ref,
    shift_ref,
    tokens_ref,
    cand_ref,
    live_at,
    pooled,
    sems,
):
    queries, length, _ = states_ref.shape
    groups = queries // GROUP
    rows = GROUP * length
    chunk = decoder_ref.shape[1]
    always = start_ref[0] >= 0
    copies = []

    def bring(source, target):
        copy = pltpu.make_async_copy(source, target, sems.at[len(copies)])
        copies.append(copy)
        copy.start()

    half = pl.ds(0, GROUP)
    other = pl.ds(GROUP, queries - GROUP)
    bring(tokens_hbm, tokens_ref)
    bring(bias_hbm, bias_ref.at[0])
    bring(gain_hbm, gain_ref.at[0])
    bring(shift_hbm, shift_ref.at[0])
    bring(states_hbm.at[half], states_ref.at[half])
    bring(transform_hbm, transform_ref)
    early = len(copies)
    bring(decoder_hbm.at[:, pl.ds(0, chunk)], decoder_ref)
    bring(decoder_bias_hbm, decoder_bias_ref.at[0])
    bring(states_hbm.at[other], states_ref.at[other])
    bring(cand_hbm, cand_ref)
    middle = len(copies)

    def normed(group):
        at = group * GROUP
        normed_ref[group * rows : (group + 1) * rows, :] = normed_rows(
            states_ref[at : at + GROUP],
            live_at[...],
            at,
            transform_ref[...],
            bias_ref[...],
            gain_ref[...],
            shift_ref[...],
        )

    for copy in copies[:early]:
        copy.wait()

    @pl.when(always)
    def _():
        place_of(rows, live_at, tokens_ref)
        normed(0)

    for copy in copies[early:middle]:
        copy.wait()
    bring(decoder_hbm.at[:, pl.ds(chunk, next_ref.shape[1])], next_ref)

    @pl.when(always)
    def _():
        for group in range(groups):
            if group + 1 < groups:
                normed(group + 1)
            part = normed_ref[group * rows : (group + 1) * rows, :]
            pool(part, decoder_ref, decoder_bias_ref[:, :chunk], group, length, pooled)
        out_ref[:, :chunk] = keep_vocab(start_ref[0], pooled)
        depth = cand_ref.shape[0]
        wide = jnp.concatenate([cand_ref[...].astype(F32), jnp.zeros((depth, LANES - queries), F32)], axis=1)
        if depth < queries:
            wide = jnp.concatenate([wide, jnp.zeros((queries - depth, LANES), F32)], axis=0)
        out_ref[:, chunk:] = wide.astype(BF16)

    copies[-1].wait()


def chunk_kernel(begin, start_ref, normed_ref, decoder_ref, decoder_bias_ref, out_ref, pooled):
    queries, chunk = pooled.shape
    rows = normed_ref.shape[0] * GROUP // queries
    for group in range(queries // GROUP):
        part = normed_ref[group * rows : (group + 1) * rows, :]
        bias = decoder_bias_ref[:, begin : begin + chunk]
        pool(part, decoder_ref, bias, group, rows // GROUP, pooled)
    out_ref[...] = keep_vocab(start_ref[0] + begin, pooled)


def slot_queries(cand, base, tile_total):
    depth, queries = cand.shape
    row = lax.broadcasted_iota(jnp.int32, (tile_total, queries), 0) + base
    hits = jnp.zeros((tile_total, queries), F32)
    for place in range(depth):
        hits = jnp.where(cand[place : place + 1, :] == row, 1.0, hits)
    hits = hits.astype(BF16)
    mine = lax.broadcasted_iota(jnp.int32, (queries, queries), 0)
    other = lax.broadcasted_iota(jnp.int32, (queries, queries), 1)
    last = (((1,), (1,)), ((), ()))
    turned = lax.dot_general(
        jnp.where(mine == other, 1.0, 0.0).astype(BF16), hits, last, preferred_element_type=F32
    )
    before = lax.dot_general(
        jnp.where(other < mine, 1.0, 0.0).astype(BF16), hits, last, preferred_element_type=F32
    )
    rank = jnp.where(turned > 0.0, before, -1.0).astype(BF16)
    slots = tile_total * MOST
    tile = lax.broadcasted_iota(jnp.int32, (tile_total, slots), 0)
    spread = jnp.where(lax.broadcasted_iota(jnp.int32, (tile_total, slots), 1) // MOST == tile, 1.0, 0.0)
    wide = jnp.dot(rank, spread.astype(BF16), preferred_element_type=F32)
    want = (lax.broadcasted_iota(jnp.int32, (queries, slots), 1) % MOST).astype(F32)
    query = lax.broadcasted_iota(jnp.int32, (queries, slots), 0)
    return jnp.sum(jnp.where(wide == want, query, 0), axis=0, keepdims=True)


def docs_copies(far_ref, begin, target, sems):
    tile_total, blocks, _, _ = target.shape
    part = pl.ds(begin, blocks)
    return [
        pltpu.make_async_copy(far_ref.at[tile, part], target.at[tile], sems.at[tile]) for tile in range(tile_total)
    ]


def gather_weights(weight_refs, turned):
    queries = weight_refs[0].shape[0]
    for party, ref in enumerate(weight_refs):
        turned[party * queries : (party + 1) * queries, :] = ref[:, : turned.shape[1]]


def step_scores(step, begin, occupancy_ref, docs_ref, turned):
    tiles = LANES // MOST
    left = [
        jnp.concatenate(
            [
                jnp.where(occupancy_ref[tile, begin + block] != 0, docs_ref[tile, block], 0.0).astype(BF16)
                for block in range(docs_ref.shape[1])
            ],
            axis=1,
        )
        for tile in range(step * tiles, (step + 1) * tiles)
    ]
    return lax.dot_general(
        jnp.concatenate(left, axis=0), turned[...], (((1,), (1,)), ((), ())), preferred_element_type=F32
    )


def first_score_kernel(parties, depth, place_ref, occupancy_ref, far_ref, *refs):
    weight_refs = refs[:parties]
    after_ref, next_ref, slots_ref, turned, docs_ref, own_sems, next_sems = refs[parties:]
    tile_total, blocks, docs, _ = docs_ref.shape
    tiles = LANES // MOST
    rows = tiles * docs
    queries, chunk = weight_refs[0].shape[0], turned.shape[1]
    always = place_ref[0] >= 0
    own = docs_copies(far_ref, 0, docs_ref, own_sems)
    later = docs_copies(far_ref, blocks, next_ref, next_sems)
    queue = own + later

    def start(number):
        for copy in queue[:number]:
            copy.start()
        del queue[:number]

    start(3 * tiles)

    @pl.when(always)
    def _():
        gather_weights(weight_refs, turned)
        for party, ref in enumerate(weight_refs):
            cand = ref[:depth, chunk : chunk + queries].astype(F32).astype(jnp.int32)
            found = slot_queries(cand, place_ref[0] * tile_total, tile_total)
            slots_ref[party : party + 1, :] = found + party * queries % LANES

    start(2 * tiles)
    for step in range(tile_total // tiles):
        for copy in own[step * tiles : (step + 1) * tiles]:
            copy.wait()
        start(2 * tiles)

        @pl.when(always)
        def _(step=step):
            after_ref[step * rows : (step + 1) * rows, :] = step_scores(step, 0, occupancy_ref, docs_ref, turned)

    start(len(queue))
    for copy in later:
        copy.wait()


def last_score_kernel(begin, parties, place_ref, occupancy_ref, docs_ref, before_ref, slots_ref, *refs):
    weight_refs = refs[:parties]
    out_ref, turned, total = refs[parties:]
    tile_total, _, docs, _ = docs_ref.shape
    tiles = LANES // MOST
    rows = tiles * docs
    queries = weight_refs[0].shape[0]
    term_count, share = total.shape[1], docs // total.shape[1]
    gather_weights(weight_refs, turned)
    lane = lax.broadcasted_iota(jnp.int32, (docs, LANES), 1) // MOST
    for step in range(tile_total // tiles):
        value = before_ref[step * rows : (step + 1) * rows, :]
        value = value + step_scores(step, begin, occupancy_ref, docs_ref, turned)
        for party in range(parties):
            column = party * queries // LANES * LANES
            source = slots_ref[party : party + 1, step * LANES : (step + 1) * LANES]
            source = jnp.broadcast_to(source, (docs, LANES))
            part = None
            for tile in range(tiles):
                held = value[tile * docs : (tile + 1) * docs, column : column + LANES]
                held = jnp.take_along_axis(held, source, axis=1, mode="promise_in_bounds")
                part = held if part is None else jnp.where(lane == tile, held, part)
            for term in range(term_count):
                total[party, term, step * share : (step + 1) * share, :] = part[term * share : (term + 1) * share]
    for party in range(parties):
        out_ref[:, place_ref[0] ^ party] = total[party].astype(BF16)


def ranks(cand, row, queries):
    depth, total = cand.shape
    hits = jnp.zeros((row.shape[0], total), F32)
    for place in range(depth):
        hits = jnp.where(cand[place : place + 1, :] == row, 1.0, hits)
    earlier = lax.broadcasted_iota(jnp.int32, (total, total), 0)
    later = lax.broadcasted_iota(jnp.int32, (total, total), 1)
    before = jnp.dot(
        hits.astype(BF16), jnp.where(earlier < later, 1.0, 0.0).astype(BF16), preferred_element_type=F32
    )
    return jnp.where(hits > 0.0, before, -1.0)


def choice_kernel(cand_ref, out_ref):
    queries = cand_ref.shape[1]
    groups = out_ref.shape[0]
    tiles = LANES // MOST
    cand = cand_ref[...]
    rank = ranks(cand, lax.broadcasted_iota(jnp.int32, (groups * tiles, queries), 0), queries)
    slot = lax.broadcasted_iota(jnp.int32, (LANES, tiles * queries), 0)
    for group in range(groups):
        want = [rank[group * tiles + k : group * tiles + k + 1] for k in range(tiles)]
        want = [jnp.where(w >= 0.0, w + k * MOST, -1.0) for k, w in enumerate(want)]
        want = jnp.concatenate(want, axis=1).astype(jnp.int32)
        out_ref[group] = jnp.where(slot == want, 1.0, 0.0).astype(BF16)


def final_kernel(cand_ref, choice_ref, got_ref, out_ref):
    term_count, docs_n, rows, _ = got_ref.shape
    depth, share, queries = out_ref.shape
    groups = rows // share
    tiles = LANES // MOST
    cand = cand_ref[...]
    twice = jnp.concatenate([cand, cand], axis=1)
    lane = lax.broadcasted_iota(jnp.int32, (1, 2 * queries), 1) // queries
    result = [jnp.zeros((share, 2 * queries), F32) for _ in range(depth)]
    for doc in range(docs_n):
        summed = got_ref[0, doc].astype(F32)
        for term in range(1, term_count):
            summed = summed + got_ref[term, doc].astype(F32)
        for group in range(groups):
            first = (doc * groups + group) * tiles
            value = summed[group * share : (group + 1) * share]
            high = value.astype(BF16)
            low = (value - high.astype(F32)).astype(BF16)
            both = jnp.concatenate([high, low], axis=0)
            moved = jnp.dot(both, choice_ref[doc * groups + group], preferred_element_type=F32)
            moved = moved[:share] + moved[share:]
            for pair in range(tiles // 2):
                held = moved[:, pair * 2 * queries : (pair + 1) * 2 * queries]
                name = first + pair * 2 + lane
                for place in range(depth):
                    result[place] = jnp.where(twice[place : place + 1] == name, held, result[place])
    for place in range(depth):
        out_ref[place] = result[place][:, :queries] + result[place][:, queries:]


def body(
    query_states,
    token_ids,
    transform_weight,
    transform_bias,
    norm_gain,
    norm_bias,
    decoder_weight,
    decoder_bias,
    candidates,
    occupancy,
    doc_blocks,
):
    query_count, length, width = query_states.shape
    vocab = decoder_weight.shape[1]
    tile_local, blocks, docs, terms = doc_blocks.shape
    depth = candidates.shape[1]
    term_index, doc_index = lax.axis_index("term"), lax.axis_index("doc")
    doc_count, term_count = lax.axis_size("doc"), lax.axis_size("term")
    share = docs // term_count
    all_queries = doc_count * query_count
    tiles = LANES // MOST
    steps = tile_local // tiles
    cuts = (0, blocks // 2, blocks)
    few = [cuts[k + 1] - cuts[k] for k in range(2)]
    chunks = [count * terms for count in few]
    begins = [cut * terms for cut in cuts[:2]]
    cand = candidates.T
    start = (term_index * vocab).reshape(1)
    place = doc_index.reshape(1)
    rows = query_count * length
    far, near = pltpu.HBM, pltpu.VMEM

    def put(space, *operands):
        return [pltpu.with_memory_space_constraint(operand, space) for operand in operands]

    def call(name, kernel, in_specs, out_shape, scratch, macs, limit, operands):
        return pl.pallas_call(
            kernel,
            in_specs=in_specs,
            out_specs=jax.tree.map(lambda _: WHOLE, out_shape),
            out_shape=out_shape,
            scratch_shapes=scratch,
            cost_estimate=pl.CostEstimate(flops=2 * macs, bytes_accessed=10**6, transcendentals=0),
            compiler_params=pltpu.CompilerParams(vmem_limit_bytes=limit),
            name=name,
        )(*operands)

    def next_docs(at):
        return near((tile_local, few[at], docs, terms), BF16)

    def pooled(at):
        return pltpu.VMEM((query_count, chunks[at]), F32)

    def turned(at):
        return pltpu.VMEM((all_queries, chunks[at]), BF16)

    def piece(at):
        return jax.ShapeDtypeStruct((query_count, chunks[at]), BF16)

    signals = pltpu.SemaphoreType.DMA((tile_local,))
    running = near((tile_local * docs, all_queries), F32)
    expand_macs = [rows * width * chunk for chunk in chunks]
    score_macs = [4 * tile_local * docs * chunk * all_queries for chunk in chunks]
    xor = [[(i, i ^ k) for i in range(doc_count)] for k in range(doc_count)]

    def spread(own, after):
        held = [own] + [None] * (doc_count - 1)
        bit, known = doc_count // 2, [0]
        while bit:
            for k in list(known):
                held[k | bit] = lax.ppermute(held[k], "doc", xor[bit])
                known.append(k | bit)
            if bit == doc_count // 2:
                held[bit], _ = lax.optimization_barrier((held[bit], after))
            bit //= 2
        return held

    first, normed, decoder, all_bias = call(
        "expand_first",
        first_kernel,
        [SCALARS] + [FAR] * 9,
        [
            jax.ShapeDtypeStruct((query_count, chunks[0] + LANES), BF16),
            near((rows, width), BF16),
            near((width, chunks[1]), BF16),
            near((1, vocab), F32),
        ],
        [
            pltpu.VMEM(query_states.shape, BF16),
            pltpu.VMEM(transform_weight.shape, BF16),
            pltpu.VMEM((width, chunks[0]), BF16),
            pltpu.VMEM((1, width), F32),
            pltpu.VMEM((1, width), F32),
            pltpu.VMEM((1, width), F32),
            pltpu.VMEM((length, query_count), jnp.int32),
            pltpu.VMEM(cand.shape, jnp.int32),
            pltpu.VMEM((GROUP * length, query_count), F32),
            pooled(0),
            pltpu.SemaphoreType.DMA((11,)),
        ],
        rows * width * width + expand_macs[0],
        16 << 20,
        [start]
        + put(
            far,
            query_states,
            token_ids.T,
            transform_weight,
            transform_bias,
            norm_gain,
            norm_bias,
            decoder_weight,
            decoder_bias,
            cand,
        ),
    )
    last = call(
        "expand_last",
        functools.partial(chunk_kernel, begins[1]),
        [SCALARS] + [WHOLE] * 3,
        piece(1),
        [pooled(1)],
        expand_macs[1],
        7 << 20,
        [start, *put(near, normed, decoder, all_bias)],
    )
    first_all = spread(first, last)
    scores, near_docs, slots = call(
        "score_first",
        functools.partial(first_score_kernel, doc_count, depth),
        [SCALARS] * 2 + [FAR] + [WHOLE] * doc_count,
        [running, next_docs(1), near((doc_count, tile_local * MOST), jnp.int32)],
        [turned(0), pltpu.VMEM((tile_local, few[0], docs, terms), BF16), signals, signals],
        score_macs[0],
        20 << 20,
        [place, occupancy, *put(far, doc_blocks), *first_all],
    )
    last_all = spread(last, scores)
    sent = call(
        "score_last",
        functools.partial(last_score_kernel, cuts[1], doc_count),
        [SCALARS] * 2 + [WHOLE] * (3 + doc_count),
        jax.ShapeDtypeStruct((term_count, doc_count, steps * share, LANES), BF16),
        [turned(1), pltpu.VMEM((doc_count, term_count, steps * share, LANES), F32)],
        score_macs[1],
        8 << 20,
        [place, occupancy, *put(near, near_docs, scores, slots), *last_all],
    )
    weights = jnp.concatenate([first[:, : chunks[0]], last], axis=1)

    everyone = doc_count * term_count
    got = lax.all_to_all(
        sent.reshape(everyone, steps * share, LANES), ("term", "doc"), split_axis=0, concat_axis=0, tiled=True
    ).reshape(term_count, doc_count, steps * share, LANES)
    choices = call(
        "choices",
        choice_kernel,
        [WHOLE],
        jax.ShapeDtypeStruct((doc_count * steps, LANES, tiles * query_count), BF16),
        [],
        10**6,
        8 << 20,
        [cand],
    )
    scores = call(
        "place",
        final_kernel,
        [WHOLE] * 3,
        jax.ShapeDtypeStruct((depth, share, query_count), F32),
        [],
        10**6,
        8 << 20,
        [cand, choices, got],
    )
    return weights, scores.transpose(2, 0, 1)


def solution(mesh):
    placed = (
        P("doc", None, None),
        P("doc", None),
        P(),
        P(),
        P(),
        P(),
        P(None, "term"),
        P("term"),
        P("doc", None),
        P("doc", "term"),
        P("doc", "term", None, None),
    )
    return jax.shard_map(
        body,
        mesh=mesh,
        in_specs=placed,
        out_specs=(P("doc", "term"), P("doc", None, "term")),
        check_vma=False,
    )
```

```python
import functools
import math

import jax
import jax.numpy as jnp
from jax import lax
from jax.experimental import pallas as pl
from jax.experimental.pallas import tpu as pltpu
from jax.sharding import PartitionSpec as P

VOCAB = 30522
MOST = 32
LANES = 128
GROUP = 8
F32 = jnp.float32
BF16 = jnp.bfloat16
WHOLE = pl.BlockSpec(memory_space=pltpu.VMEM)
FAR = pl.BlockSpec(memory_space=pltpu.HBM)
SCALARS = pl.BlockSpec(memory_space=pltpu.SMEM)


def gelu(value):
    return 0.5 * value * (1.0 + lax.erf(value * math.sqrt(0.5)))


def normed_rows(states, live_at, first, transform, bias, gain, shift):
    queries, length, width = states.shape
    rows = queries * length
    row = lax.broadcasted_iota(jnp.int32, live_at.shape, 0)
    lane = lax.broadcasted_iota(jnp.int32, live_at.shape, 1)
    own = jnp.where(lane == first + row % queries, live_at, 0.0)
    live = jnp.sum(own, axis=1, keepdims=True) > 0.0
    row = lax.broadcasted_iota(jnp.int32, (rows, 1), 0)
    source = row % queries * length + jnp.where(live, row // queries, 0)
    column = lax.broadcasted_iota(jnp.int32, (rows, rows), 1)
    order = jnp.where(column == source, 1.0, 0.0).astype(BF16)
    moved = jnp.dot(order, states.reshape(rows, width), preferred_element_type=F32)
    hidden = jnp.dot(moved.astype(BF16), transform, preferred_element_type=F32)
    hidden = gelu(hidden + bias)
    centred = hidden - jnp.mean(hidden, axis=1, keepdims=True)
    spread = jnp.mean(centred * centred, axis=1, keepdims=True)
    return (centred * lax.rsqrt(spread + 1e-06) * gain + shift).astype(BF16)


def place_of(rows, live_at, tokens_ref):
    length = tokens_ref.shape[0]
    at = lax.broadcasted_iota(jnp.int32, (rows, length), 0) // GROUP
    spot = lax.broadcasted_iota(jnp.int32, (rows, length), 1)
    pick = jnp.where(at == spot, 1.0, 0.0).astype(BF16)
    alive = jnp.where(tokens_ref[...] != 0, 1.0, 0.0).astype(BF16)
    live_at[...] = jnp.dot(pick, alive, preferred_element_type=F32)


def pool(rows, decoder_ref, bias, group, length, out_ref):
    logits = jnp.dot(rows, decoder_ref[...], preferred_element_type=F32)
    top = jnp.max(logits.reshape(length, GROUP, logits.shape[1]), axis=0)
    out_ref[group * GROUP : (group + 1) * GROUP, :] = jnp.log1p(
        jnp.maximum(top + bias, 0.0)
    )


def keep_vocab(start, pooled):
    column = start + lax.broadcasted_iota(jnp.int32, pooled.shape, 1)
    return jnp.where(column < VOCAB, pooled[...], 0.0).astype(BF16)


def first_kernel(
    start_ref,
    states_hbm,
    tokens_hbm,
    transform_hbm,
    bias_hbm,
    gain_hbm,
    shift_hbm,
    decoder_hbm,
    decoder_bias_hbm,
    cand_hbm,
    out_ref,
    normed_ref,
    next_ref,
    decoder_bias_ref,
    states_ref,
    transform_ref,
    decoder_ref,
    bias_ref,
    gain_ref,
    shift_ref,
    tokens_ref,
    cand_ref,
    live_at,
    pooled,
    sems,
):
    queries, length, _ = states_ref.shape
    groups = queries // GROUP
    rows = GROUP * length
    chunk = decoder_ref.shape[1]
    always = start_ref[0] >= 0
    copies = []

    def bring(source, target):
        copy = pltpu.make_async_copy(source, target, sems.at[len(copies)])
        copies.append(copy)
        copy.start()

    half = pl.ds(0, 2 * GROUP)
    other = pl.ds(2 * GROUP, queries - 2 * GROUP)
    bring(tokens_hbm, tokens_ref)
    bring(bias_hbm, bias_ref.at[0])
    bring(gain_hbm, gain_ref.at[0])
    bring(shift_hbm, shift_ref.at[0])
    bring(states_hbm.at[half], states_ref.at[half])
    bring(transform_hbm, transform_ref)
    early = len(copies)
    bring(decoder_hbm.at[:, pl.ds(0, chunk)], decoder_ref)
    bring(decoder_bias_hbm, decoder_bias_ref.at[0])
    bring(states_hbm.at[other], states_ref.at[other])
    bring(cand_hbm, cand_ref)
    middle = len(copies)

    def normed(group):
        at = group * GROUP
        normed_ref[group * rows : (group + 1) * rows, :] = normed_rows(
            states_ref[at : at + GROUP],
            live_at[...],
            at,
            transform_ref[...],
            bias_ref[...],
            gain_ref[...],
            shift_ref[...],
        )

    for copy in copies[:early]:
        copy.wait()

    @pl.when(always)
    def _():
        place_of(rows, live_at, tokens_ref)
        normed(0)
        normed(1)

    for copy in copies[early:middle]:
        copy.wait()
    bring(decoder_hbm.at[:, pl.ds(chunk, next_ref.shape[1])], next_ref)

    @pl.when(always)
    def _():
        for group in range(groups):
            if group + 2 < groups:
                normed(group + 2)
            part = normed_ref[group * rows : (group + 1) * rows, :]
            pool(part, decoder_ref, decoder_bias_ref[:, :chunk], group, length, pooled)
        out_ref[:, :chunk] = keep_vocab(start_ref[0], pooled)
        depth = cand_ref.shape[0]
        wide = jnp.concatenate([cand_ref[...].astype(F32), jnp.zeros((depth, LANES - queries), F32)], axis=1)
        if depth < queries:
            wide = jnp.concatenate([wide, jnp.zeros((queries - depth, LANES), F32)], axis=0)
        out_ref[:, chunk:] = wide.astype(BF16)

    copies[-1].wait()


def chunk_kernel(begin, start_ref, normed_ref, decoder_ref, decoder_bias_ref, out_ref, pooled):
    queries, chunk = pooled.shape
    rows = normed_ref.shape[0] * GROUP // queries
    for group in range(queries // GROUP):
        part = normed_ref[group * rows : (group + 1) * rows, :]
        bias = decoder_bias_ref[:, begin : begin + chunk]
        pool(part, decoder_ref, bias, group, rows // GROUP, pooled)
    out_ref[...] = keep_vocab(start_ref[0] + begin, pooled)


def slot_queries(cand, base, tile_total):
    depth, queries = cand.shape
    row = lax.broadcasted_iota(jnp.int32, (tile_total, queries), 0) + base
    hits = jnp.zeros((tile_total, queries), F32)
    for place in range(depth):
        hits = jnp.where(cand[place : place + 1, :] == row, 1.0, hits)
    hits = hits.astype(BF16)
    mine = lax.broadcasted_iota(jnp.int32, (queries, queries), 0)
    other = lax.broadcasted_iota(jnp.int32, (queries, queries), 1)
    last = (((1,), (1,)), ((), ()))
    turned = lax.dot_general(
        jnp.where(mine == other, 1.0, 0.0).astype(BF16), hits, last, preferred_element_type=F32
    )
    before = lax.dot_general(
        jnp.where(other < mine, 1.0, 0.0).astype(BF16), hits, last, preferred_element_type=F32
    )
    rank = jnp.where(turned > 0.0, before, -1.0).astype(BF16)
    slots = tile_total * MOST
    tile = lax.broadcasted_iota(jnp.int32, (tile_total, slots), 0)
    spread = jnp.where(lax.broadcasted_iota(jnp.int32, (tile_total, slots), 1) // MOST == tile, 1.0, 0.0)
    wide = jnp.dot(rank, spread.astype(BF16), preferred_element_type=F32)
    want = (lax.broadcasted_iota(jnp.int32, (queries, slots), 1) % MOST).astype(F32)
    query = lax.broadcasted_iota(jnp.int32, (queries, slots), 0)
    return jnp.sum(jnp.where(wide == want, query, 0), axis=0, keepdims=True)


def docs_copies(far_ref, begin, target, sems):
    tile_total, blocks, _, _ = target.shape
    part = pl.ds(begin, blocks)
    return [
        pltpu.make_async_copy(far_ref.at[tile, part], target.at[tile], sems.at[tile]) for tile in range(tile_total)
    ]


def gather_weights(weight_refs, turned):
    queries = weight_refs[0].shape[0]
    for party, ref in enumerate(weight_refs):
        turned[party * queries : (party + 1) * queries, :] = ref[:, : turned.shape[1]]


def step_scores(step, begin, occupancy_ref, docs_ref, turned):
    tiles = LANES // MOST
    left = [
        jnp.concatenate(
            [
                jnp.where(occupancy_ref[tile, begin + block] != 0, docs_ref[tile, block], 0.0).astype(BF16)
                for block in range(docs_ref.shape[1])
            ],
            axis=1,
        )
        for tile in range(step * tiles, (step + 1) * tiles)
    ]
    return lax.dot_general(
        jnp.concatenate(left, axis=0), turned[...], (((1,), (1,)), ((), ())), preferred_element_type=F32
    )


def first_score_kernel(parties, depth, place_ref, occupancy_ref, far_ref, *refs):
    weight_refs = refs[:parties]
    after_ref, next_ref, slots_ref, turned, docs_ref, own_sems, next_sems = refs[parties:]
    tile_total, blocks, docs, _ = docs_ref.shape
    tiles = LANES // MOST
    rows = tiles * docs
    queries, chunk = weight_refs[0].shape[0], turned.shape[1]
    always = place_ref[0] >= 0
    own = docs_copies(far_ref, 0, docs_ref, own_sems)
    later = docs_copies(far_ref, blocks, next_ref, next_sems)
    queue = own + later

    def start(number):
        for copy in queue[:number]:
            copy.start()
        del queue[:number]

    start(3 * tiles)

    @pl.when(always)
    def _():
        gather_weights(weight_refs, turned)
        for party, ref in enumerate(weight_refs):
            cand = ref[:depth, chunk : chunk + queries].astype(F32).astype(jnp.int32)
            found = slot_queries(cand, place_ref[0] * tile_total, tile_total)
            slots_ref[party : party + 1, :] = found + party * queries % LANES

    start(2 * tiles)
    for step in range(tile_total // tiles):
        for copy in own[step * tiles : (step + 1) * tiles]:
            copy.wait()
        start(2 * tiles)

        @pl.when(always)
        def _(step=step):
            after_ref[step * rows : (step + 1) * rows, :] = step_scores(step, 0, occupancy_ref, docs_ref, turned)

    start(len(queue))
    for copy in later:
        copy.wait()


def last_score_kernel(begin, parties, place_ref, occupancy_ref, docs_ref, before_ref, slots_ref, *refs):
    weight_refs = refs[:parties]
    out_ref, turned, total = refs[parties:]
    tile_total, _, docs, _ = docs_ref.shape
    tiles = LANES // MOST
    rows = tiles * docs
    queries = weight_refs[0].shape[0]
    term_count, share = total.shape[1], docs // total.shape[1]
    gather_weights(weight_refs, turned)
    lane = lax.broadcasted_iota(jnp.int32, (docs, LANES), 1) // MOST
    for step in range(tile_total // tiles):
        value = before_ref[step * rows : (step + 1) * rows, :]
        value = value + step_scores(step, begin, occupancy_ref, docs_ref, turned)
        for party in range(parties):
            column = party * queries // LANES * LANES
            source = slots_ref[party : party + 1, step * LANES : (step + 1) * LANES]
            source = jnp.broadcast_to(source, (docs, LANES))
            part = None
            for tile in range(tiles):
                held = value[tile * docs : (tile + 1) * docs, column : column + LANES]
                held = jnp.take_along_axis(held, source, axis=1, mode="promise_in_bounds")
                part = held if part is None else jnp.where(lane == tile, held, part)
            for term in range(term_count):
                total[party, term, step * share : (step + 1) * share, :] = part[term * share : (term + 1) * share]
    for party in range(parties):
        out_ref[:, place_ref[0] ^ party] = total[party].astype(BF16)


def ranks(cand, row, queries):
    depth, total = cand.shape
    hits = jnp.zeros((row.shape[0], total), F32)
    for place in range(depth):
        hits = jnp.where(cand[place : place + 1, :] == row, 1.0, hits)
    earlier = lax.broadcasted_iota(jnp.int32, (total, total), 0)
    later = lax.broadcasted_iota(jnp.int32, (total, total), 1)
    before = jnp.dot(
        hits.astype(BF16), jnp.where(earlier < later, 1.0, 0.0).astype(BF16), preferred_element_type=F32
    )
    return jnp.where(hits > 0.0, before, -1.0)


def choice_kernel(cand_ref, out_ref):
    queries = cand_ref.shape[1]
    groups = out_ref.shape[0]
    tiles = LANES // MOST
    cand = cand_ref[...]
    rank = ranks(cand, lax.broadcasted_iota(jnp.int32, (groups * tiles, queries), 0), queries)
    slot = lax.broadcasted_iota(jnp.int32, (LANES, tiles * queries), 0)
    for group in range(groups):
        want = [rank[group * tiles + k : group * tiles + k + 1] for k in range(tiles)]
        want = [jnp.where(w >= 0.0, w + k * MOST, -1.0) for k, w in enumerate(want)]
        want = jnp.concatenate(want, axis=1).astype(jnp.int32)
        out_ref[group] = jnp.where(slot == want, 1.0, 0.0).astype(BF16)


def final_kernel(cand_ref, choice_ref, got_ref, out_ref):
    term_count, docs_n, rows, _ = got_ref.shape
    depth, share, queries = out_ref.shape
    groups = rows // share
    tiles = LANES // MOST
    cand = cand_ref[...]
    twice = jnp.concatenate([cand, cand], axis=1)
    lane = lax.broadcasted_iota(jnp.int32, (1, 2 * queries), 1) // queries
    result = [jnp.zeros((share, 2 * queries), F32) for _ in range(depth)]
    for doc in range(docs_n):
        summed = got_ref[0, doc].astype(F32)
        for term in range(1, term_count):
            summed = summed + got_ref[term, doc].astype(F32)
        for group in range(groups):
            first = (doc * groups + group) * tiles
            value = summed[group * share : (group + 1) * share]
            high = value.astype(BF16)
            low = (value - high.astype(F32)).astype(BF16)
            both = jnp.concatenate([high, low], axis=0)
            moved = jnp.dot(both, choice_ref[doc * groups + group], preferred_element_type=F32)
            moved = moved[:share] + moved[share:]
            for pair in range(tiles // 2):
                held = moved[:, pair * 2 * queries : (pair + 1) * 2 * queries]
                name = first + pair * 2 + lane
                for place in range(depth):
                    result[place] = jnp.where(twice[place : place + 1] == name, held, result[place])
    for place in range(depth):
        out_ref[place] = result[place][:, :queries] + result[place][:, queries:]


def body(
    query_states,
    token_ids,
    transform_weight,
    transform_bias,
    norm_gain,
    norm_bias,
    decoder_weight,
    decoder_bias,
    candidates,
    occupancy,
    doc_blocks,
):
    query_count, length, width = query_states.shape
    vocab = decoder_weight.shape[1]
    tile_local, blocks, docs, terms = doc_blocks.shape
    depth = candidates.shape[1]
    term_index, doc_index = lax.axis_index("term"), lax.axis_index("doc")
    doc_count, term_count = lax.axis_size("doc"), lax.axis_size("term")
    share = docs // term_count
    all_queries = doc_count * query_count
    tiles = LANES // MOST
    steps = tile_local // tiles
    cuts = (0, blocks // 2, blocks)
    few = [cuts[k + 1] - cuts[k] for k in range(2)]
    chunks = [count * terms for count in few]
    begins = [cut * terms for cut in cuts[:2]]
    cand = candidates.T
    start = (term_index * vocab).reshape(1)
    place = doc_index.reshape(1)
    rows = query_count * length
    far, near = pltpu.HBM, pltpu.VMEM

    def put(space, *operands):
        return [pltpu.with_memory_space_constraint(operand, space) for operand in operands]

    def call(name, kernel, in_specs, out_shape, scratch, macs, limit, operands):
        return pl.pallas_call(
            kernel,
            in_specs=in_specs,
            out_specs=jax.tree.map(lambda _: WHOLE, out_shape),
            out_shape=out_shape,
            scratch_shapes=scratch,
            cost_estimate=pl.CostEstimate(flops=2 * macs, bytes_accessed=10**6, transcendentals=0),
            compiler_params=pltpu.CompilerParams(vmem_limit_bytes=limit),
            name=name,
        )(*operands)

    def next_docs(at):
        return near((tile_local, few[at], docs, terms), BF16)

    def pooled(at):
        return pltpu.VMEM((query_count, chunks[at]), F32)

    def turned(at):
        return pltpu.VMEM((all_queries, chunks[at]), BF16)

    def piece(at):
        return jax.ShapeDtypeStruct((query_count, chunks[at]), BF16)

    signals = pltpu.SemaphoreType.DMA((tile_local,))
    running = near((tile_local * docs, all_queries), F32)
    expand_macs = [rows * width * chunk for chunk in chunks]
    score_macs = [4 * tile_local * docs * chunk * all_queries for chunk in chunks]
    xor = [[(i, i ^ k) for i in range(doc_count)] for k in range(doc_count)]

    def spread(own, after):
        held = [own] + [None] * (doc_count - 1)
        bit, known = doc_count // 2, [0]
        while bit:
            for k in list(known):
                held[k | bit] = lax.ppermute(held[k], "doc", xor[bit])
                known.append(k | bit)
            if bit == doc_count // 2:
                held[bit], _ = lax.optimization_barrier((held[bit], after))
            bit //= 2
        return held

    first, normed, decoder, all_bias = call(
        "expand_first",
        first_kernel,
        [SCALARS] + [FAR] * 9,
        [
            jax.ShapeDtypeStruct((query_count, chunks[0] + LANES), BF16),
            near((rows, width), BF16),
            near((width, chunks[1]), BF16),
            near((1, vocab), F32),
        ],
        [
            pltpu.VMEM(query_states.shape, BF16),
            pltpu.VMEM(transform_weight.shape, BF16),
            pltpu.VMEM((width, chunks[0]), BF16),
            pltpu.VMEM((1, width), F32),
            pltpu.VMEM((1, width), F32),
            pltpu.VMEM((1, width), F32),
            pltpu.VMEM((length, query_count), jnp.int32),
            pltpu.VMEM(cand.shape, jnp.int32),
            pltpu.VMEM((GROUP * length, query_count), F32),
            pooled(0),
            pltpu.SemaphoreType.DMA((11,)),
        ],
        rows * width * width + expand_macs[0],
        16 << 20,
        [start]
        + put(
            far,
            query_states,
            token_ids.T,
            transform_weight,
            transform_bias,
            norm_gain,
            norm_bias,
            decoder_weight,
            decoder_bias,
            cand,
        ),
    )
    last = call(
        "expand_last",
        functools.partial(chunk_kernel, begins[1]),
        [SCALARS] + [WHOLE] * 3,
        piece(1),
        [pooled(1)],
        expand_macs[1],
        7 << 20,
        [start, *put(near, normed, decoder, all_bias)],
    )
    first_all = spread(first, last)
    scores, near_docs, slots = call(
        "score_first",
        functools.partial(first_score_kernel, doc_count, depth),
        [SCALARS] * 2 + [FAR] + [WHOLE] * doc_count,
        [running, next_docs(1), near((doc_count, tile_local * MOST), jnp.int32)],
        [turned(0), pltpu.VMEM((tile_local, few[0], docs, terms), BF16), signals, signals],
        score_macs[0],
        20 << 20,
        [place, occupancy, *put(far, doc_blocks), *first_all],
    )
    last_all = spread(last, scores)
    sent = call(
        "score_last",
        functools.partial(last_score_kernel, cuts[1], doc_count),
        [SCALARS] * 2 + [WHOLE] * (3 + doc_count),
        jax.ShapeDtypeStruct((term_count, doc_count, steps * share, LANES), BF16),
        [turned(1), pltpu.VMEM((doc_count, term_count, steps * share, LANES), F32)],
        score_macs[1],
        8 << 20,
        [place, occupancy, *put(near, near_docs, scores, slots), *last_all],
    )
    weights = jnp.concatenate([first[:, : chunks[0]], last], axis=1)

    everyone = doc_count * term_count
    got = lax.all_to_all(
        sent.reshape(everyone, steps * share, LANES), ("term", "doc"), split_axis=0, concat_axis=0, tiled=True
    ).reshape(term_count, doc_count, steps * share, LANES)
    choices = call(
        "choices",
        choice_kernel,
        [WHOLE],
        jax.ShapeDtypeStruct((doc_count * steps, LANES, tiles * query_count), BF16),
        [],
        10**6,
        8 << 20,
        [cand],
    )
    scores = call(
        "place",
        final_kernel,
        [WHOLE] * 3,
        jax.ShapeDtypeStruct((depth, share, query_count), F32),
        [],
        10**6,
        8 << 20,
        [cand, choices, got],
    )
    return weights, scores.transpose(2, 0, 1)


def solution(mesh):
    placed = (
        P("doc", None, None),
        P("doc", None),
        P(),
        P(),
        P(),
        P(),
        P(None, "term"),
        P("term"),
        P("doc", None),
        P("doc", "term"),
        P("doc", "term", None, None),
    )
    return jax.shard_map(
        body,
        mesh=mesh,
        in_specs=placed,
        out_specs=(P("doc", "term"), P("doc", None, "term")),
        check_vma=False,
    )
```
